128 devices in a mesh: orient: 16 (over x, y), frame: 8 (over z, core).
Axes of the slice: x: 4, y: 4, z: 4, core: 2. Of those that a mesh axis runs over, the one named last changes fastest.
Arguments:
- counts: int32 [4096, 16384], P(('orient', 'frame')), may hold values from 0 to 8191, as said below
- pixel_gain: float32 [16384], replicated, may hold values from 0.5 to 2
- slices: bfloat16 [8192, 16384], P('orient'), may hold values from 0.25 to 8
- voxel_index: int32 [8192, 128], P('orient'), may hold values from 0 to 6143
- interp: float32 [8192, 128], P('orient'), may hold values from 0.1 to 1
Outputs:
- model: float32 [6144, 128], P(('orient', 'frame'))
The draws below stay inside these ranges and needn't reach their ends.
Inputs may be any that keep to these rules, and one draw needn't show every extreme that they name: In each frame the counts lie below 2 to the power of a level of the frame's own between 6 and 13; the first frame's level is 13 and its first pixel holds 8191.
All inputs are finite; a program needn't handle non-finite values.
Results may differ from the reference program's by a relative error of at most 0.012.
Values may be sent and summed in bfloat16 or wider, within the bound.
A program may use at most 192 MiB of HBM per device.

```python
import math
import jax
import jax.numpy as jnp
from jax import lax

NPIX = 16384
PBLK = 128
ORI_DEV = 512
ORIENTS = 8192
FRAMES = 4096
VBLOCKS = 6144
N_ORIENT = 16


def count_values(key):
    key = jax.random.fold_in(key, 11)
    level_key, power_key, count_key = jax.random.split(key, 3)
    rows = jnp.arange(FRAMES)[:, None]
    cols = jnp.arange(NPIX)[None, :]
    levels = jax.random.randint(level_key, (FRAMES, 1), 6, 14)
    levels = jnp.where(rows == 0, 13, levels)
    powers = jax.random.randint(power_key, (FRAMES, NPIX), 0, levels + 1)
    ceiling = jnp.left_shift(jnp.ones((FRAMES, NPIX), jnp.int32), powers)
    drawn = jax.random.randint(count_key, (FRAMES, NPIX), 0, ceiling)
    return jnp.where((rows == 0) & (cols == 0), 8191, drawn)


def draw_counts(key, part):
    values = count_values(key)
    return values


def draw_slices(key, part):
    key = jax.random.fold_in(key, 12)
    unit_key = jax.random.fold_in(key, 0)
    unit = jax.random.uniform(unit_key, (ORIENTS, NPIX), jnp.float32)
    low_end = math.log(0.25)
    high_end = math.log(4.0)
    return jnp.exp(low_end + unit * (high_end - low_end)).astype(jnp.bfloat16)


def with_ends(values, stream_key, smallest, high):
    place = [jax.random.randint(jax.random.fold_in(stream_key, axis), (), 0, length) for axis, length in enumerate(values.shape)]
    widest = values.shape.index(max(values.shape))
    neighbour = place[:widest] + [(place[widest] + 1) % values.shape[widest]] + place[widest + 1:]
    return values.at[tuple(place)].set(smallest).at[tuple(neighbour)].set(high)


def shard_levels(rng, dims, shards, least, top_value):
    def one(dim, parts):
        draws = jax.random.uniform(jax.random.fold_in(jax.random.fold_in(rng, 6), dim), (parts,), jnp.float32, least / len(shards), top_value / len(shards))
        return jnp.repeat(jnp.exp(draws), dims[dim] // parts).reshape((-1,) + (1,) * (len(dims) - dim - 1))

    loudness = one(*shards[0])
    for cut in shards[1:]:
        loudness = loudness * one(*cut)
    return loudness


def setup_inputs(seed: int = 0) -> dict:
    key_of = jax.random.split(jax.random.key(seed), 6)
    counts = draw_counts(jax.random.fold_in(key_of[5], 71), 0)
    pixel_gain = jnp.clip(jnp.exp(jax.random.uniform(key_of[1], (NPIX,), jnp.float32, math.log(0.5), math.log(2.0))), 0.5, 2.0)
    slices = draw_slices(jax.random.fold_in(key_of[5], 71), 0)
    voxel_index = with_ends(jax.random.randint(key_of[3], (ORIENTS, PBLK), 0, VBLOCKS), jax.random.fold_in(key_of[3], 1), 0, VBLOCKS - 1).astype(jnp.int32)
    interp = jnp.clip(jnp.exp(math.log(1.0) - 2.3025851 * jax.random.uniform(key_of[4], (ORIENTS, PBLK), jnp.float32) ** shard_levels(key_of[4], (ORIENTS, PBLK), ((0, 16),), -0.2, 0.2)), 0.1, 1.0)
    return {"counts": counts, "pixel_gain": pixel_gain, "slices": slices, "voxel_index": voxel_index, "interp": interp}


score_beta = 1.5


def reference(counts, pixel_gain, slices, voxel_index, interp):
    frames = (counts.astype(jnp.float32) * pixel_gain[None, :]).astype(jnp.bfloat16)
    photons = jnp.sum(frames.astype(jnp.float32), axis=1)
    log_slices = jnp.log(slices.astype(jnp.float32)).astype(jnp.bfloat16)
    log_mean = jnp.log(jnp.sum(slices.astype(jnp.float32), axis=1) / NPIX)
    score_scale = score_beta / NPIX
    products = lax.dot_general(frames, log_slices, (((1,), (1,)), ((), ())), preferred_element_type=jnp.float32)
    scores = (products - photons[:, None] * log_mean[None, :]) * score_scale
    frame_peak = jnp.max(scores, axis=1, keepdims=True)
    shifted = jnp.exp(scores - frame_peak)
    probability = shifted / jnp.sum(shifted, axis=1, keepdims=True)
    prob_bf = probability.astype(jnp.bfloat16)
    level = photons / NPIX
    orient_mass = jnp.sum(probability * level[:, None], axis=0)
    prob_blocks = prob_bf.T.reshape(N_ORIENT, ORI_DEV, FRAMES)
    mass_blocks = orient_mass.reshape(N_ORIENT, ORI_DEV)
    slice_blocks = slices.reshape(N_ORIENT, ORI_DEV, NPIX)
    index_blocks = voxel_index.reshape(N_ORIENT, ORI_DEV, PBLK)
    weight_blocks = interp.reshape(N_ORIENT, ORI_DEV, PBLK)

    def accumulate(carry, pieces):
        voxel_sum, voxel_weight = carry
        prob_block, mass_block, slice_block, index_block, weight_block = pieces
        gathered = jnp.dot(prob_block, frames, preferred_element_type=jnp.float32)
        updated = (gathered + 0.25 * slice_block.astype(jnp.float32)) / (mass_block + 0.25)[:, None]
        weighted = updated.reshape(ORI_DEV, PBLK, 128) * weight_block[:, :, None]
        flat_index = index_block.reshape(-1)
        voxel_sum = voxel_sum + jax.ops.segment_sum(weighted.reshape(-1, 128), flat_index, num_segments=VBLOCKS)
        voxel_weight = voxel_weight + jax.ops.segment_sum(weight_block.reshape(-1), flat_index, num_segments=VBLOCKS)
        return (voxel_sum, voxel_weight), None

    start = (jnp.zeros((VBLOCKS, 128), jnp.float32), jnp.zeros((VBLOCKS,), jnp.float32))
    (voxel_sum, voxel_weight), unused = lax.scan(accumulate, start, (prob_blocks, mass_blocks, slice_blocks, index_blocks, weight_blocks))
    return voxel_sum / (1.0 + voxel_weight)[:, None]
```

```python
import functools

import jax
import jax.numpy as jnp
from jax import lax
from jax.experimental import pallas as pl
from jax.experimental.pallas import tpu as pltpu
from jax.sharding import PartitionSpec as P

VB_DEV = 48
ACCS = 4

score_beta = 1.5


def scatter_kernel(q_count, block_ref, rows_ref, index_hbm, out_ref, index_smem, sem, *accs):
    copy = pltpu.make_async_copy(index_hbm, index_smem, sem)
    copy.start()
    voxels = out_ref.shape[0]
    orients = rows_ref.shape[1]

    def clear(t, carry):
        for acc in accs:
            acc[pl.ds(pl.multiple_of(t * 64, 64), 64), :] = jnp.zeros((64, 128), jnp.float32)
        return carry

    lax.fori_loop(0, voxels // 64, clear, 0)
    copy.wait()
    base = block_ref[0] * q_count

    def step(t, carry):
        n = 0
        for q in range(q_count):
            for s in range(8):
                r = t * 8 + s
                i = index_smem[r, base + q]
                acc = accs[n % len(accs)]
                n += 1
                acc[pl.ds(i, 1), :] += rows_ref[q, pl.ds(r, 1), :]
        return carry

    lax.fori_loop(0, orients // 8, step, 0)

    def finish(t, carry):
        d = pl.ds(pl.multiple_of(t * 64, 64), 64)
        total = accs[0][d, :]
        for acc in accs[1:]:
            total = total + acc[d, :]
        out_ref[d, :] = total
        return carry

    lax.fori_loop(0, voxels // 64, finish, 0)


def scatter(rows, index, block, voxels):
    q_count = rows.shape[0]
    return pl.pallas_call(
        functools.partial(scatter_kernel, q_count),
        out_shape=jax.ShapeDtypeStruct((voxels, 128), jnp.float32),
        in_specs=[
            pl.BlockSpec(memory_space=pltpu.SMEM),
            pl.BlockSpec(memory_space=pltpu.VMEM),
            pl.BlockSpec(memory_space=pl.ANY),
        ],
        out_specs=pl.BlockSpec(memory_space=pltpu.VMEM),
        scratch_shapes=[pltpu.SMEM(index.shape, jnp.int32), pltpu.SemaphoreType.DMA]
        + [pltpu.VMEM((voxels, 128), jnp.float32)] * ACCS,
        compiler_params=pltpu.CompilerParams(vmem_limit_bytes=48 * 2**20),
    )(block, rows, index)


def local(counts, pixel_gain, slices, voxel_index, interp):
    frame_size = lax.axis_size("frame")
    orient_size = lax.axis_size("orient")
    me = lax.axis_index("frame")
    pixel_count = slices.shape[1]
    orient_count = slices.shape[0]
    part = pixel_count // frame_size
    q_count = part // 128
    voxels = VB_DEV * orient_size * frame_size
    own = (counts.astype(jnp.float32) * pixel_gain[None, :]).astype(jnp.bfloat16)
    column = lax.all_to_all(own, "frame", split_axis=1, concat_axis=0, tiled=True)
    frames = lax.all_gather(column, "orient", axis=0, tiled=True)
    log_mean = jnp.log(jnp.sum(slices, axis=1, dtype=jnp.float32) / pixel_count)
    slice_part = lax.dynamic_slice_in_dim(slices, me * part, part, axis=1).astype(jnp.float32)
    log_slices = jnp.log(slice_part).astype(jnp.bfloat16)
    photons_part = jnp.sum(frames, axis=1, dtype=jnp.float32)
    score_scale = score_beta / pixel_count
    products = lax.dot_general(
        frames, log_slices, (((1,), (1,)), ((), ())), preferred_element_type=jnp.float32
    )
    partial = (products - photons_part[:, None] * log_mean[None, :]) * score_scale
    scores = lax.psum_scatter(partial, "frame", scatter_dimension=0, tiled=True)
    photons = lax.psum_scatter(photons_part, "frame", scatter_dimension=0, tiled=True)
    frame_peak = lax.pmax(jnp.max(scores, axis=1), "orient")
    shifted = jnp.exp(scores - frame_peak[:, None])
    frame_total = lax.psum(jnp.sum(shifted, axis=1), "orient")
    probability = shifted / frame_total[:, None]
    mass = lax.psum(jnp.sum(probability * (photons / pixel_count)[:, None], axis=0), "frame")
    prob = lax.all_gather(probability.astype(jnp.bfloat16), "frame", axis=0, tiled=True)
    gathered = lax.dot_general(
        prob, frames, (((0,), (0,)), ((), ())), preferred_element_type=jnp.float32
    )
    index = voxel_index
    weight = lax.dynamic_slice_in_dim(interp, me * q_count, q_count, axis=1)
    share = weight / (mass + 0.25)[:, None]
    rows = (gathered + 0.25 * slice_part).reshape(orient_count, q_count, 128).transpose(1, 0, 2)
    rows = rows * share.T[:, :, None]
    block = jnp.full((1,), me, jnp.int32)
    voxel_sum = scatter(rows, index, block, voxels)
    targets = lax.dynamic_slice_in_dim(voxel_index, me * q_count, q_count, axis=1).reshape(1, -1)
    flat_weight = weight.reshape(1, -1)
    upper, lower = targets // VB_DEV, targets % VB_DEV
    hot_upper = (upper == lax.broadcasted_iota(jnp.int32, (128, 1), 0)).astype(jnp.float32)
    hot_lower = jnp.where(lower == lax.broadcasted_iota(jnp.int32, (VB_DEV, 1), 0), flat_weight, 0.0)
    voxel_weight = lax.dot_general(
        hot_upper, hot_lower, (((1,), (1,)), ((), ())), precision=lax.Precision.HIGHEST
    ).reshape(-1)
    summed, weight_sum = (
        lax.psum_scatter(voxel_sum, ("orient", "frame"), scatter_dimension=0, tiled=True),
        lax.psum_scatter(voxel_weight, ("orient", "frame"), scatter_dimension=0, tiled=True),
    )
    return summed / (1.0 + weight_sum)[:, None]


def solution(mesh):
    placed = (
        P(("orient", "frame"), None),
        P(),
        P("orient", None),
        P("orient", None),
        P("orient", None),
    )
    return jax.shard_map(
        local, mesh=mesh, in_specs=placed, out_specs=P(("orient", "frame"), None), check_vma=False
    )
```

```python
import functools

import jax
import jax.numpy as jnp
from jax import lax
from jax.experimental import pallas as pl
from jax.experimental.pallas import tpu as pltpu
from jax.sharding import PartitionSpec as P

VB_DEV = 48
ACCS = 4

score_beta = 1.5


SIDE = 4
ORDERS = ((0, 1, 2), (1, 2, 0), (2, 0, 1))


def here():
    orient, frame = lax.axis_index("orient"), lax.axis_index("frame")
    return (orient // SIDE, orient % SIDE, frame // 2, frame % 2)


def device(place):
    x, y, z, core = place
    return (x * SIDE + y, z * 2 + core)


def moved(place, axis, step):
    out = list(place)
    out[axis] = (place[axis] + step) % SIDE
    return tuple(out)


def pick(ref, axis, value, ndim):
    return ref.at[tuple(value if a == axis else slice(None) for a in range(ndim))]


def sums_kernel(v_ref, w_ref, o_ref, pair_out, pair_in, s1, s1b, in1, s2, s2b, in2, s3, s3b, in3,
                wsum, wpair_in, win1, w2, win2, w3, win3,
                pair_sem, sem1, sem2, sem3, wpair_sem, wsem1, wsem2, wsem3):
    me = here()
    core = me[3]
    sibling = (me[0], me[1], me[2], 1 - core)
    barrier = pltpu.get_barrier_semaphore()
    peers = [sibling] + [moved(me, a, d) for a in range(3) for d in (1, 2, 3)]
    for peer in peers:
        pl.semaphore_signal(barrier, inc=1, device_id=device(peer), device_id_type=pl.DeviceIdType.MESH)
    for p in range(3):
        pair_out[p] = v_ref[:, :, :, 1 - core, 16 * p:16 * p + 16, :].astype(jnp.bfloat16)
    pl.semaphore_wait(barrier, len(peers))

    def send(src, dst, sems, slot, place):
        copy = pltpu.make_async_remote_copy(
            src_ref=src, dst_ref=dst, send_sem=sems.at[0, slot], recv_sem=sems.at[1, slot],
            device_id=device(place), device_id_type=pl.DeviceIdType.MESH)
        copy.start()
        return copy

    pair = [send(pair_out.at[p], pair_in.at[p], pair_sem, p, sibling) for p in range(3)]
    wpair = send(w_ref.at[1 - core], wpair_in, wpair_sem, 0, sibling)
    first, second, third = [], [], []
    for p in range(3):
        axis = ORDERS[p][0]
        pair[p].wait_recv()
        total = v_ref[:, :, :, core, 16 * p:16 * p + 16, :] + pair_in[p].astype(jnp.float32)
        s1[p] = total
        s1b[p] = total.astype(jnp.bfloat16)
        first.append([send(pick(s1b.at[p], axis, (me[axis] + d) % SIDE, 3), in1.at[p, d - 1], sem1, 3 * p + d - 1,
                           moved(me, axis, d)) for d in (1, 2, 3)])
    wpair.wait_recv()
    wsum[...] = w_ref[core] + wpair_in[...]
    wfirst = [send(wsum.at[(me[0] + d) % SIDE], win1.at[d - 1], wsem1, d - 1, moved(me, 0, d)) for d in (1, 2, 3)]
    for p in range(3):
        axis, nxt = ORDERS[p][0], ORDERS[p][1]
        for copy in first[p]:
            copy.wait_recv()
        own = pick(s1.at[p], axis, me[axis], 3)[...]
        total = own + in1[p, 0].astype(jnp.float32) + in1[p, 1].astype(jnp.float32) + in1[p, 2].astype(jnp.float32)
        s2[p] = total
        s2b[p] = total.astype(jnp.bfloat16)
        dim = nxt - (1 if nxt > axis else 0)
        second.append([send(pick(s2b.at[p], dim, (me[nxt] + d) % SIDE, 2), in2.at[p, d - 1], sem2, 3 * p + d - 1,
                            moved(me, nxt, d)) for d in (1, 2, 3)])
    for copy in wfirst:
        copy.wait_recv()
    w2[...] = wsum[me[0]] + win1[0] + win1[1] + win1[2]
    wsecond = [send(w2, win2.at[d - 1], wsem2, d - 1, moved(me, 1, d)) for d in (1, 2, 3)]
    for p in range(3):
        axis, nxt, last = ORDERS[p]
        for copy in second[p]:
            copy.wait_recv()
        dim = nxt - (1 if nxt > axis else 0)
        own = pick(s2.at[p], dim, me[nxt], 2)[...]
        total = own + in2[p, 0].astype(jnp.float32) + in2[p, 1].astype(jnp.float32) + in2[p, 2].astype(jnp.float32)
        s3[p] = total
        s3b[p] = total.astype(jnp.bfloat16)
        third.append([send(s3b.at[p, (me[last] + d) % SIDE], in3.at[p, d - 1], sem3, 3 * p + d - 1,
                           moved(me, last, d)) for d in (1, 2, 3)])
    for copy in wsecond:
        copy.wait_recv()
    w3[...] = w2[...] + win2[0] + win2[1] + win2[2]
    wthird = [send(w3, win3.at[d - 1], wsem3, d - 1, moved(me, 2, d)) for d in (1, 2, 3)]
    for copy in wthird:
        copy.wait_recv()
    weights = w3[...] + win3[0] + win3[1] + win3[2]
    mine = lax.broadcasted_iota(jnp.int32, weights.shape, 0) == me[1] * SIDE + me[2]
    row = jnp.sum(jnp.where(mine, weights, 0.0), axis=0, keepdims=True)
    shape = (o_ref.shape[0], 128)
    diagonal = lax.broadcasted_iota(jnp.int32, shape, 0) == lax.broadcasted_iota(jnp.int32, shape, 1)
    column = jnp.sum(jnp.where(diagonal, row, 0.0), axis=1, keepdims=True)
    scale = 1.0 / (1.0 + column)
    for p in range(3):
        for copy in third[p]:
            copy.wait_recv()
        own = s3[p, me[ORDERS[p][2]]]
        total = own + in3[p, 0].astype(jnp.float32) + in3[p, 1].astype(jnp.float32) + in3[p, 2].astype(jnp.float32)
        o_ref[16 * p:16 * p + 16, :] = total * scale[16 * p:16 * p + 16]
    for copies in pair, [wpair], *first, *second, *third, wfirst, wsecond, wthird:
        for copy in copies:
            copy.wait_send()


def reduce_blocks(voxel_sum, voxel_weight):
    f32, b16 = jnp.float32, jnp.bfloat16
    vm, dma = pltpu.VMEM, pltpu.SemaphoreType.DMA
    scratch = [
        vm((3, 4, 4, 4, 16, 128), b16), vm((3, 4, 4, 4, 16, 128), b16),
        vm((3, 4, 4, 4, 16, 128), f32), vm((3, 4, 4, 4, 16, 128), b16), vm((3, 3, 4, 4, 16, 128), b16),
        vm((3, 4, 4, 16, 128), f32), vm((3, 4, 4, 16, 128), b16), vm((3, 3, 4, 16, 128), b16),
        vm((3, 4, 16, 128), f32), vm((3, 4, 16, 128), b16), vm((3, 3, 16, 128), b16),
        vm((4, 16, 128), f32), vm((4, 16, 128), f32), vm((3, 16, 128), f32),
        vm((16, 128), f32), vm((3, 16, 128), f32), vm((16, 128), f32), vm((3, 16, 128), f32),
        dma((2, 3)), dma((2, 9)), dma((2, 9)), dma((2, 9)), dma((2, 1)), dma((2, 3)), dma((2, 3)), dma((2, 3)),
    ]
    vspec = pl.BlockSpec(memory_space=pltpu.VMEM)
    return pl.pallas_call(
        sums_kernel,
        out_shape=jax.ShapeDtypeStruct((48, 128), f32),
        in_specs=[vspec, vspec], out_specs=vspec, scratch_shapes=scratch,
        compiler_params=pltpu.CompilerParams(collective_id=3, has_side_effects=True, vmem_limit_bytes=40 * 2**20),
    )(voxel_sum, voxel_weight)


def scatter_kernel(q_count, block_ref, rows_ref, index_hbm, out_ref, index_smem, sem, *accs):
    copy = pltpu.make_async_copy(index_hbm, index_smem, sem)
    copy.start()
    voxels = out_ref.shape[0]
    orients = rows_ref.shape[1]

    def clear(t, carry):
        for acc in accs:
            acc[pl.ds(pl.multiple_of(t * 64, 64), 64), :] = jnp.zeros((64, 128), jnp.float32)
        return carry

    lax.fori_loop(0, voxels // 64, clear, 0)
    copy.wait()
    base = block_ref[0] * q_count

    def step(t, carry):
        n = 0
        for q in range(q_count):
            for s in range(8):
                r = t * 8 + s
                i = index_smem[r, base + q]
                acc = accs[n % len(accs)]
                n += 1
                acc[pl.ds(i, 1), :] += rows_ref[q, pl.ds(r, 1), :]
        return carry

    lax.fori_loop(0, orients // 8, step, 0)

    def finish(t, carry):
        d = pl.ds(pl.multiple_of(t * 64, 64), 64)
        total = accs[0][d, :]
        for acc in accs[1:]:
            total = total + acc[d, :]
        out_ref[d, :] = total
        return carry

    lax.fori_loop(0, voxels // 64, finish, 0)


def scatter(rows, index, block, voxels):
    q_count = rows.shape[0]
    return pl.pallas_call(
        functools.partial(scatter_kernel, q_count),
        out_shape=jax.ShapeDtypeStruct((voxels, 128), jnp.float32),
        in_specs=[
            pl.BlockSpec(memory_space=pltpu.SMEM),
            pl.BlockSpec(memory_space=pltpu.VMEM),
            pl.BlockSpec(memory_space=pl.ANY),
        ],
        out_specs=pl.BlockSpec(memory_space=pltpu.VMEM),
        scratch_shapes=[pltpu.SMEM(index.shape, jnp.int32), pltpu.SemaphoreType.DMA]
        + [pltpu.VMEM((voxels, 128), jnp.float32)] * ACCS,
        compiler_params=pltpu.CompilerParams(vmem_limit_bytes=48 * 2**20),
    )(block, rows, index)


def local(counts, pixel_gain, slices, voxel_index, interp):
    frame_size = lax.axis_size("frame")
    orient_size = lax.axis_size("orient")
    me = lax.axis_index("frame")
    pixel_count = slices.shape[1]
    orient_count = slices.shape[0]
    part = pixel_count // frame_size
    q_count = part // 128
    voxels = VB_DEV * orient_size * frame_size
    own = (counts.astype(jnp.float32) * pixel_gain[None, :]).astype(jnp.bfloat16)
    column = lax.all_to_all(own, "frame", split_axis=1, concat_axis=0, tiled=True)
    frames = lax.all_gather(column, "orient", axis=0, tiled=True)
    log_mean = jnp.log(jnp.sum(slices, axis=1, dtype=jnp.float32) / pixel_count)
    slice_part = lax.dynamic_slice_in_dim(slices, me * part, part, axis=1).astype(jnp.float32)
    log_slices = jnp.log(slice_part).astype(jnp.bfloat16)
    photons_part = jnp.sum(frames, axis=1, dtype=jnp.float32)
    score_scale = score_beta / pixel_count
    products = lax.dot_general(
        frames, log_slices, (((1,), (1,)), ((), ())), preferred_element_type=jnp.float32
    )
    partial = (products - photons_part[:, None] * log_mean[None, :]) * score_scale
    scores = lax.psum_scatter(partial, "frame", scatter_dimension=0, tiled=True)
    photons = lax.psum_scatter(photons_part, "frame", scatter_dimension=0, tiled=True)
    frame_peak = lax.pmax(jnp.max(scores, axis=1), "orient")
    shifted = jnp.exp(scores - frame_peak[:, None])
    frame_total = lax.psum(jnp.sum(shifted, axis=1), "orient")
    probability = shifted / frame_total[:, None]
    mass = lax.psum(jnp.sum(probability * (photons / pixel_count)[:, None], axis=0), "frame")
    prob = lax.all_gather(probability.astype(jnp.bfloat16), "frame", axis=0, tiled=True)
    gathered = lax.dot_general(
        prob, frames, (((0,), (0,)), ((), ())), preferred_element_type=jnp.float32
    )
    index = voxel_index
    weight = lax.dynamic_slice_in_dim(interp, me * q_count, q_count, axis=1)
    share = weight / (mass + 0.25)[:, None]
    rows = (gathered + 0.25 * slice_part).reshape(orient_count, q_count, 128).transpose(1, 0, 2)
    rows = rows * share.T[:, :, None]
    block = jnp.full((1,), me, jnp.int32)
    voxel_sum = scatter(rows, index, block, voxels)
    targets = lax.dynamic_slice_in_dim(voxel_index, me * q_count, q_count, axis=1).reshape(1, -1)
    flat_weight = weight.reshape(1, -1)
    upper, lower = targets // VB_DEV, targets % VB_DEV
    slot = lax.broadcasted_iota(jnp.int32, (128, 1), 0)
    owner = 2 * (slot % 64) + slot // 64
    hot_upper = (upper == owner).astype(jnp.float32)
    hot_lower = jnp.where(lower == slot, flat_weight, 0.0)
    voxel_weight = lax.dot_general(
        hot_upper, hot_lower, (((1,), (1,)), ((), ())), precision=lax.Precision.HIGHEST
    )
    return reduce_blocks(
        voxel_sum.reshape(SIDE, SIDE, SIDE, 2, VB_DEV, 128), voxel_weight.reshape(2, SIDE, SIDE * SIDE, 128)
    )


def solution(mesh):
    placed = (
        P(("orient", "frame"), None),
        P(),
        P("orient", None),
        P("orient", None),
        P("orient", None),
    )
    return jax.shard_map(
        local, mesh=mesh, in_specs=placed, out_specs=P(("orient", "frame"), None), check_vma=False
    )
```

```python
import functools

import jax
import jax.numpy as jnp
from jax import lax
from jax.experimental import pallas as pl
from jax.experimental.pallas import tpu as pltpu
from jax.sharding import PartitionSpec as P

VB_DEV = 48
ACCS = 4


SIDE = 4
ORDERS = ((0, 1, 2), (1, 2, 0), (2, 0, 1))


def here():
    orient, frame = lax.axis_index("orient"), lax.axis_index("frame")
    return (orient // SIDE, orient % SIDE, frame // 2, frame % 2)


def device(place):
    x, y, z, core = place
    return (x * SIDE + y, z * 2 + core)


def moved(place, axis, step):
    out = list(place)
    out[axis] = (place[axis] + step) % SIDE
    return tuple(out)


def pick(ref, axis, value, ndim):
    return ref.at[tuple(value if a == axis else slice(None) for a in range(ndim))]


def sums_kernel(v_ref, w_ref, o_ref, pair_out, pair_in, s1, s1b, in1, s2, s2b, in2, s3, s3b, in3,
                wsum, wpair_in, win1, w2, win2, w3, win3,
                pair_sem, sem1, sem2, sem3, wpair_sem, wsem1, wsem2, wsem3):
    me = here()
    core = me[3]
    sibling = (me[0], me[1], me[2], 1 - core)
    barrier = pltpu.get_barrier_semaphore()
    peers = [sibling] + [moved(me, a, d) for a in range(3) for d in (1, 2, 3)]
    for peer in peers:
        pl.semaphore_signal(barrier, inc=1, device_id=device(peer), device_id_type=pl.DeviceIdType.MESH)
    for p in range(3):
        pair_out[p] = v_ref[:, :, :, 1 - core, 16 * p:16 * p + 16, :].astype(jnp.bfloat16)
    pl.semaphore_wait(barrier, len(peers))

    def send(src, dst, sems, slot, place):
        copy = pltpu.make_async_remote_copy(
            src_ref=src, dst_ref=dst, send_sem=sems.at[0, slot], recv_sem=sems.at[1, slot],
            device_id=device(place), device_id_type=pl.DeviceIdType.MESH)
        copy.start()
        return copy

    pair = [send(pair_out.at[p], pair_in.at[p], pair_sem, p, sibling) for p in range(3)]
    wpair = send(w_ref.at[1 - core], wpair_in, wpair_sem, 0, sibling)
    first, second, third = [], [], []
    for p in range(3):
        axis = ORDERS[p][0]
        pair[p].wait_recv()
        total = v_ref[:, :, :, core, 16 * p:16 * p + 16, :] + pair_in[p].astype(jnp.float32)
        s1[p] = total
        s1b[p] = total.astype(jnp.bfloat16)
        first.append([send(pick(s1b.at[p], axis, (me[axis] + d) % SIDE, 3), in1.at[p, d - 1], sem1, 3 * p + d - 1,
                           moved(me, axis, d)) for d in (1, 2, 3)])
    wpair.wait_recv()
    wsum[...] = w_ref[core] + wpair_in[...]
    wfirst = [send(wsum.at[(me[0] + d) % SIDE], win1.at[d - 1], wsem1, d - 1, moved(me, 0, d)) for d in (1, 2, 3)]
    for p in range(3):
        axis, nxt = ORDERS[p][0], ORDERS[p][1]
        for copy in first[p]:
            copy.wait_recv()
        own = pick(s1.at[p], axis, me[axis], 3)[...]
        total = own + in1[p, 0].astype(jnp.float32) + in1[p, 1].astype(jnp.float32) + in1[p, 2].astype(jnp.float32)
        s2[p] = total
        s2b[p] = total.astype(jnp.bfloat16)
        dim = nxt - (1 if nxt > axis else 0)
        second.append([send(pick(s2b.at[p], dim, (me[nxt] + d) % SIDE, 2), in2.at[p, d - 1], sem2, 3 * p + d - 1,
                            moved(me, nxt, d)) for d in (1, 2, 3)])
    for copy in wfirst:
        copy.wait_recv()
    w2[...] = wsum[me[0]] + win1[0] + win1[1] + win1[2]
    wsecond = [send(w2, win2.at[d - 1], wsem2, d - 1, moved(me, 1, d)) for d in (1, 2, 3)]
    for p in range(3):
        axis, nxt, last = ORDERS[p]
        for copy in second[p]:
            copy.wait_recv()
        dim = nxt - (1 if nxt > axis else 0)
        own = pick(s2.at[p], dim, me[nxt], 2)[...]
        total = own + in2[p, 0].astype(jnp.float32) + in2[p, 1].astype(jnp.float32) + in2[p, 2].astype(jnp.float32)
        s3[p] = total
        s3b[p] = total.astype(jnp.bfloat16)
        third.append([send(s3b.at[p, (me[last] + d) % SIDE], in3.at[p, d - 1], sem3, 3 * p + d - 1,
                           moved(me, last, d)) for d in (1, 2, 3)])
    for copy in wsecond:
        copy.wait_recv()
    w3[...] = w2[...] + win2[0] + win2[1] + win2[2]
    wthird = [send(w3, win3.at[d - 1], wsem3, d - 1, moved(me, 2, d)) for d in (1, 2, 3)]
    for copy in wthird:
        copy.wait_recv()
    weights = w3[...] + win3[0] + win3[1] + win3[2]
    mine = lax.broadcasted_iota(jnp.int32, weights.shape, 0) == me[1] * SIDE + me[2]
    row = jnp.sum(jnp.where(mine, weights, 0.0), axis=0, keepdims=True)
    shape = (o_ref.shape[0], 128)
    diagonal = lax.broadcasted_iota(jnp.int32, shape, 0) == lax.broadcasted_iota(jnp.int32, shape, 1)
    column = jnp.sum(jnp.where(diagonal, row, 0.0), axis=1, keepdims=True)
    scale = 1.0 / (1.0 + column)
    for p in range(3):
        for copy in third[p]:
            copy.wait_recv()
        own = s3[p, me[ORDERS[p][2]]]
        total = own + in3[p, 0].astype(jnp.float32) + in3[p, 1].astype(jnp.float32) + in3[p, 2].astype(jnp.float32)
        o_ref[16 * p:16 * p + 16, :] = total * scale[16 * p:16 * p + 16]
    for copies in pair, [wpair], *first, *second, *third, wfirst, wsecond, wthird:
        for copy in copies:
            copy.wait_send()


def reduce_blocks(voxel_sum, voxel_weight):
    f32, b16 = jnp.float32, jnp.bfloat16
    vm, dma = pltpu.VMEM, pltpu.SemaphoreType.DMA
    scratch = [
        vm((3, 4, 4, 4, 16, 128), b16), vm((3, 4, 4, 4, 16, 128), b16),
        vm((3, 4, 4, 4, 16, 128), f32), vm((3, 4, 4, 4, 16, 128), b16), vm((3, 3, 4, 4, 16, 128), b16),
        vm((3, 4, 4, 16, 128), f32), vm((3, 4, 4, 16, 128), b16), vm((3, 3, 4, 16, 128), b16),
        vm((3, 4, 16, 128), f32), vm((3, 4, 16, 128), b16), vm((3, 3, 16, 128), b16),
        vm((4, 16, 128), f32), vm((4, 16, 128), f32), vm((3, 16, 128), f32),
        vm((16, 128), f32), vm((3, 16, 128), f32), vm((16, 128), f32), vm((3, 16, 128), f32),
        dma((2, 3)), dma((2, 9)), dma((2, 9)), dma((2, 9)), dma((2, 1)), dma((2, 3)), dma((2, 3)), dma((2, 3)),
    ]
    vspec = pl.BlockSpec(memory_space=pltpu.VMEM)
    return pl.pallas_call(
        sums_kernel,
        out_shape=jax.ShapeDtypeStruct((48, 128), f32),
        in_specs=[vspec, vspec], out_specs=vspec, scratch_shapes=scratch,
        compiler_params=pltpu.CompilerParams(collective_id=3, has_side_effects=True, vmem_limit_bytes=40 * 2**20),
    )(voxel_sum, voxel_weight)


PARTS = 8
PART = 2048
HALF = 256
HELD = 272
score_beta = 1.5
NT = (((1,), (1,)), ((), ()))


def iterate_kernel(counts_ref, gain_ref, interp_ref, slices_hbm, rows_ref,
                   own, frames, part, stream, logs, log_mean, scores, pair_in, blocks, z1_in, kept, z2_in,
                   shifted, photon, stat, stat2, stat3, sib_in, x_in, y_in, prob, gathered, mass,
                   load_sem, a2a_send, a2a_recv, g_send, g_recv, pair_sem, z1_sem, z2_sem, sib_sem,
                   x_send, x_recv, y_send, y_recv, ag1_sem, ag2_sem, agc_sem):
    f32, b16 = jnp.float32, jnp.bfloat16
    x, y, z, core = me = here()
    plane = z * 2 + core
    pixel_count = PARTS * PART
    sibling = (x, y, z, 1 - core)
    near = (x, y, z + 1 - 2 * (z % 2), core)
    far = (x, y, 3 - z, core)
    group = ((z + 1) // 2) % 2
    spot = z // 2
    xl, xr, yl, yr = (x + 3) % 4, (x + 1) % 4, (y + 3) % 4, (y + 1) % 4
    to_xr, to_xl = (xr, y, z, core), (xl, y, z, core)
    to_yr, to_yl = (x, yr, z, core), (x, yl, z, core)

    def remote(src, dst, send_sem, recv_sem, place):
        return pltpu.make_async_remote_copy(
            src_ref=src, dst_ref=dst, send_sem=send_sem, recv_sem=recv_sem,
            device_id=device(place), device_id_type=pl.DeviceIdType.MESH)

    def when(s, body, limit=PARTS):
        pl.when((s >= 0) & (s < limit))(lambda: body(s))

    load = pltpu.make_async_copy(
        slices_hbm.at[:, pl.ds(pl.multiple_of(plane * PART, PART), PART)], part, load_sem.at[0])
    load.start()

    def stream_copy(j):
        return pltpu.make_async_copy(
            slices_hbm.at[pl.ds(pl.multiple_of(core * HALF, HALF), HALF), pl.ds(pl.multiple_of(j * PART, PART), PART)],
            stream.at[j % 2], load_sem.at[1 + j % 2])

    stream_copy(0).start()
    stream_copy(1).start()

    barrier = pltpu.get_barrier_semaphore()
    column = [(plane + d) % PARTS for d in range(1, PARTS)]
    peers = [(x, y, k // 2, k % 2) for k in column]
    peers += [moved(me, 0, d) for d in (1, 2, 3)] + [moved(me, 1, d) for d in (1, 2, 3)]
    for peer in peers:
        pl.semaphore_signal(barrier, inc=1, device_id=device(peer), device_id_type=pl.DeviceIdType.MESH)

    def correct(j, carry):
        lanes = pl.ds(pl.multiple_of(j * PART, PART), PART)
        own[j] = (counts_ref[:, lanes].astype(f32) * gain_ref[:, lanes]).astype(b16)
        return carry

    lax.fori_loop(0, PARTS, correct, 0)
    frames[plane, x, y] = own[plane]
    pl.semaphore_wait(barrier, len(peers))

    def a2a_copy(d):
        k = (plane + d) % PARTS
        return remote(own.at[k], frames.at[plane, x, y], a2a_send.at[d - 1], a2a_recv.at[plane], (x, y, k // 2, k % 2))

    def a2a_start(d, carry):
        a2a_copy(d).start()
        return carry

    lax.fori_loop(1, PARTS, a2a_start, 0)

    def order(i):
        return jnp.where(i == 0, plane, jnp.where(i - 1 < plane, i - 1, i))

    def gather_copy(i, n):
        s = order(i)
        lo, hi = pl.ds(0, 16), pl.ds(16, 16)
        left, right = pl.ds(0, PART // 2), pl.ds(PART // 2, PART // 2)
        two, other = pl.ds(0, 2), pl.ds(2, 2)
        every = pl.ds(0, 4)
        full = pl.ds(0, PART)
        where, place = [
            ((s, x, y, lo, full), to_xr), ((s, x, y, lo, full), to_xl),
            ((s, x, y, hi, full), to_yr), ((s, x, y, hi, full), to_yl),
            ((s, xl, y, lo, left), to_xr), ((s, xr, y, lo, right), to_xl),
            ((s, x, yl, hi, left), to_yr), ((s, x, yr, hi, right), to_yl),
            ((s, every, y, lo, full), to_yr), ((s, every, y, lo, full), to_yl),
            ((s, x, every, hi, full), to_xr), ((s, x, every, hi, full), to_xl),
            ((s, two, yl, lo, full), to_yr), ((s, other, yr, lo, full), to_yl),
            ((s, xl, two, hi, full), to_xr), ((s, xr, other, hi, full), to_xl),
        ][n]
        return remote(frames.at[where], frames.at[where], g_send.at[i, n], g_recv.at[i, n], place)

    def gather(stage):
        def body(i):
            if stage == 1:
                s = order(i)

                @pl.when(s != plane)
                def _():
                    remote(own.at[0], frames.at[s, x, y], a2a_send.at[0], a2a_recv.at[s], sibling).wait_recv()
            else:
                for n in range(4 * stage - 8, 4 * stage - 4):
                    gather_copy(i, n).wait_recv()
            if stage < 5:
                for n in range(4 * stage - 4, 4 * stage):
                    gather_copy(i, n).start()
        return body

    when(0, gather(1))

    log_mean[...] = jnp.zeros_like(log_mean)

    def add_means(j, carry):
        stream_copy(j).wait()
        log_mean[...] += jnp.dot(stream[j % 2], jnp.ones((PART, 128), b16), preferred_element_type=f32)

        @pl.when(j + 2 < PARTS)
        def _():
            stream_copy(j + 2).start()
        return carry

    lax.fori_loop(0, PARTS, add_means, 0)
    log_mean[...] = jnp.log(log_mean[...] / pixel_count)
    gather(2)(0)
    load.wait()

    def take_logs(h):
        def body(j, carry):
            rows = pl.ds(pl.multiple_of(j * 16, 16), 16)
            logs[h, rows, :] = jnp.log(part[pl.ds(pl.multiple_of(h * HALF + j * 16, 16), 16), :].astype(f32)).astype(b16)
            return carry
        lax.fori_loop(0, HALF // 16, body, 0)
        logs[h, HALF:HELD, :] = jnp.ones((HELD - HALF, PART), b16)

    take_logs(0)
    gather(3)(0)
    gather(1)(1)
    take_logs(1)
    gather(2)(1)
    gather(1)(2)
    weight = interp_ref[...]
    weight_hi = weight.astype(b16)
    weight_lo = (weight - weight_hi.astype(f32)).astype(b16)

    def spread(j, carry):
        lane = lax.broadcasted_iota(jnp.int32, (128, 256), 0)
        column_of = plane * 16 + 2 * j + lax.broadcasted_iota(jnp.int32, (128, 256), 1) // 128
        hot = jnp.where(lane == column_of, 1.0, 0.0).astype(b16)
        out = jnp.dot(weight_hi, hot, preferred_element_type=f32) + jnp.dot(weight_lo, hot, preferred_element_type=f32)
        rows_ref[2 * j] = out[:, :128]
        rows_ref[2 * j + 1] = out[:, 128:]
        return carry

    lax.fori_loop(0, PARTS, spread, 0)
    mass[...] = jnp.zeros_like(mass)

    def clear(j, carry):
        gathered[pl.ds(pl.multiple_of(j * 16, 16), 16), :] = jnp.zeros((16, PART), f32)
        return carry

    lax.fori_loop(0, 2 * HALF // 16, clear, 0)

    def pair_copy(s):
        return remote(scores.at[s % 2, 1 - core], pair_in.at[s], pair_sem.at[0, s], pair_sem.at[1, s], sibling)

    def z1_copy(s):
        return remote(blocks.at[s % 2, 1 - group], z1_in.at[s], z1_sem.at[0, s], z1_sem.at[1, s], near)

    def z2_copy(s):
        return remote(kept.at[s % 2, 1 - spot], z2_in.at[s], z2_sem.at[0, s], z2_sem.at[1, s], far)

    def sib_copy(s):
        return remote(stat.at[s % 2], sib_in.at[s], sib_sem.at[0, s], sib_sem.at[1, s], sibling)

    def x_copy(s, d):
        return remote(stat2.at[s % 2], x_in.at[s, d - 1], x_send.at[s, d - 1], x_recv.at[s, d - 1], moved(me, 0, d))

    def y_copy(s, d):
        return remote(stat3.at[s % 2], y_in.at[s, d - 1], y_send.at[s, d - 1], y_recv.at[s, d - 1], moved(me, 1, d))

    def ag1_copy(s):
        lanes = pl.ds(pl.multiple_of(z * 128, 128), 128)
        return remote(prob.at[s, core, :, lanes], prob.at[s, core, :, lanes], ag1_sem.at[0, s], ag1_sem.at[1, s], near)

    def ag2_copy(s):
        lanes = pl.ds(pl.multiple_of(spot * 256, 256), 256)
        return remote(prob.at[s, core, :, lanes], prob.at[s, core, :, lanes], ag2_sem.at[0, s], ag2_sem.at[1, s], far)

    def agc_copy(s):
        return remote(prob.at[s, core], prob.at[s, core], agc_sem.at[0, s], agc_sem.at[1, s], sibling)

    def multiply(s):
        pl.when(s >= 2)(lambda: pair_copy(s - 2).wait_send())

        def tile(j, carry):
            block = frames[s, pl.ds(2 * j, 2)].reshape(HALF, PART)
            lanes = pl.ds(pl.multiple_of(j * HALF, HALF), HALF)
            for h in range(2):
                scores[s % 2, h, :, lanes] = lax.dot_general(logs[h], block, NT, preferred_element_type=f32)
            return carry

        lax.fori_loop(0, 2, tile, 0)
        pair_copy(s).start()

    def add_pair(s):
        pl.when(s >= 2)(lambda: z1_copy(s - 2).wait_send())
        pair_copy(s).wait_recv()
        for b, (g, n) in enumerate(((0, 0), (1, 0), (1, 1), (0, 1))):
            lanes = slice(128 * b, 128 * b + 128)
            blocks[s % 2, g, n] = scores[s % 2, core, :, lanes] + pair_in[s, :, lanes]
        z1_copy(s).start()

    def add_near(s):
        pl.when(s >= 2)(lambda: z2_copy(s - 2).wait_send())
        z1_copy(s).wait_recv()
        kept[s % 2] = blocks[s % 2, group] + z1_in[s]
        z2_copy(s).start()

    first_row = lax.broadcasted_iota(jnp.int32, (8, 128), 0) == 0

    def combine(tiles):
        peak = tiles[0][0:1]
        for tile in tiles[1:]:
            peak = jnp.maximum(peak, tile[0:1])
        total = sum(tile[1:2] * jnp.exp(tile[0:1] - peak) for tile in tiles)
        return peak, total

    def score(s):
        pl.when(s >= 2)(lambda: sib_copy(s - 2).wait_send())
        z2_copy(s).wait_recv()
        total = kept[s % 2, spot] + z2_in[s]
        photons = total[HALF:HALF + 1]
        value = (total[:HALF] - photons * log_mean[...]) * (score_beta / pixel_count)
        peak = jnp.max(value, axis=0, keepdims=True)
        value = jnp.exp(value - peak)
        shifted[s % 2] = value
        photon[s % 2] = jnp.broadcast_to(photons, (8, 128))
        stat[s % 2] = jnp.where(first_row, peak, jnp.sum(value, axis=0, keepdims=True))
        sib_copy(s).start()

    def add_sibling(s):
        pl.when(s >= 2)(lambda: [x_copy(s - 2, d).wait_send() for d in (1, 2, 3)] and None)
        sib_copy(s).wait_recv()
        peak, total = combine([stat[s % 2], sib_in[s]])
        stat2[s % 2] = jnp.where(first_row, peak, total)
        for d in (1, 2, 3):
            x_copy(s, d).start()

    def add_x(s):
        pl.when(s >= 2)(lambda: [y_copy(s - 2, d).wait_send() for d in (1, 2, 3)] and None)
        for d in (1, 2, 3):
            x_copy(s, d).wait_recv()
        peak, total = combine([stat2[s % 2], x_in[s, 0], x_in[s, 1], x_in[s, 2]])
        stat3[s % 2] = jnp.where(first_row, peak, total)
        for d in (1, 2, 3):
            y_copy(s, d).start()

    def normalise(s):
        for d in (1, 2, 3):
            y_copy(s, d).wait_recv()
        peak, total = combine([stat3[s % 2], y_in[s, 0], y_in[s, 1], y_in[s, 2]])
        factor = jnp.exp(stat[s % 2][0:1] - peak) / total
        lanes = pl.ds(pl.multiple_of(z * 128, 128), 128)
        prob[s, core, :HALF, lanes] = (shifted[s % 2] * factor).astype(b16)
        photons = photon[s % 2][0:1]
        upper = photons.astype(b16).astype(f32)
        row = lax.broadcasted_iota(jnp.int32, (HELD - HALF, 128), 0)
        prob[s, core, HALF:, lanes] = jnp.where(row == 0, upper, jnp.where(row == 1, photons - upper, 0.0)).astype(b16)
        ag1_copy(s).start()

    def spread_near(s):
        ag1_copy(s).wait_recv()
        ag2_copy(s).start()

    def spread_far(s):
        ag2_copy(s).wait_recv()
        agc_copy(s).start()

    def gather_pixels(s):
        agc_copy(s).wait_recv()
        for h in range(2):
            mass[h] += lax.dot_general(prob[s, h, :HALF], prob[s, 0, HALF:], NT, preferred_element_type=f32)

        def tile(j, carry):
            lanes = pl.ds(pl.multiple_of(j * 256, 256), 256)
            block = frames[s, :, :, :, lanes].reshape(2 * HALF, 256)
            for h in range(2):
                gathered[h * HALF:h * HALF + HALF, lanes] += jnp.dot(prob[s, h, :HALF], block, preferred_element_type=f32)
            return carry

        lax.fori_loop(0, PARTS, tile, 0)

    def tick(t, carry):
        when(t + 2, gather(3))
        when(t + 3, gather(2))
        when(t + 4, gather(1))
        when(t + 1, gather(4))
        when(t, gather(5))
        when(t - 1, multiply)
        when(t - 2, score)
        when(t - 3, spread_near)
        when(t - 1, add_pair)
        when(t - 2, add_sibling)
        when(t - 3, spread_far)
        when(t - 2, add_x)
        when(t - 1, add_near)
        when(t - 2, normalise)
        when(t - 3, gather_pixels)
        return carry

    lax.fori_loop(-1, PARTS + 3, tick, 0)

    share = 1.0 / (jnp.sum(mass[...], axis=2, keepdims=True) * (1.0 / pixel_count) + 0.25)
    for q in range(PART // 128):
        for h in range(2):
            lanes, some = slice(128 * q, 128 * q + 128), slice(h * HALF, h * HALF + HALF)
            rows_ref[q, some] = rows_ref[q, some] * (
                (gathered[some, lanes] + 0.25 * part[some, lanes].astype(f32)) * share[h])

    def drain(i, carry):
        for n in range(16):
            gather_copy(i, n).wait_send()
        ag1_copy(i).wait_send()
        ag2_copy(i).wait_send()
        agc_copy(i).wait_send()
        return carry

    lax.fori_loop(0, PARTS, drain, 0)

    def drain_a2a(d, carry):
        a2a_copy(d).wait_send()
        return carry

    lax.fori_loop(1, PARTS, drain_a2a, 0)
    for s in (PARTS - 2, PARTS - 1):
        pair_copy(s).wait_send()
        z1_copy(s).wait_send()
        z2_copy(s).wait_send()
        sib_copy(s).wait_send()
        for d in (1, 2, 3):
            x_copy(s, d).wait_send()
            y_copy(s, d).wait_send()


def iterate(counts, gain, interp, slices):
    f32, b16 = jnp.float32, jnp.bfloat16
    vm, dma = pltpu.VMEM, pltpu.SemaphoreType.DMA
    n = PARTS
    scratch = [
        vm((n, 32, PART), b16), vm((n, 4, 4, 32, PART), b16), vm((2 * HALF, PART), b16), vm((2, HALF, PART), b16),
        vm((2, HELD, PART), b16), vm((HALF, 128), f32), vm((2, 2, HELD, 512), f32), vm((n, HELD, 512), f32),
        vm((2, 2, 2, HELD, 128), f32), vm((n, 2, HELD, 128), f32), vm((2, 2, HELD, 128), f32), vm((n, HELD, 128), f32),
        vm((2, HALF, 128), f32), vm((2, 8, 128), f32), vm((2, 8, 128), f32), vm((2, 8, 128), f32), vm((2, 8, 128), f32),
        vm((n, 8, 128), f32), vm((n, 3, 8, 128), f32), vm((n, 3, 8, 128), f32),
        vm((n, 2, HELD, 512), b16), vm((2 * HALF, PART), f32), vm((2, HALF, HELD - HALF), f32),
        dma((3,)), dma((n - 1,)), dma((n,)), dma((n, 16)), dma((n, 16)), dma((2, n)), dma((2, n)), dma((2, n)), dma((2, n)),
        dma((n, 3)), dma((n, 3)), dma((n, 3)), dma((n, 3)), dma((2, n)), dma((2, n)), dma((2, n)),
    ]
    vspec, anyspec = pl.BlockSpec(memory_space=pltpu.VMEM), pl.BlockSpec(memory_space=pl.ANY)
    return pl.pallas_call(
        iterate_kernel,
        out_shape=jax.ShapeDtypeStruct((PART // 128, 2 * HALF, 128), f32),
        in_specs=[vspec, vspec, vspec, anyspec], out_specs=vspec, scratch_shapes=scratch,
        compiler_params=pltpu.CompilerParams(collective_id=2, has_side_effects=True, vmem_limit_bytes=62 * 2**20),
    )(counts, gain.reshape(1, -1), interp, slices)


def scatter_kernel(q_count, block_ref, rows_ref, index_hbm, out_ref, index_smem, sem, *accs):
    copy = pltpu.make_async_copy(index_hbm, index_smem, sem)
    copy.start()
    voxels = out_ref.shape[0]
    orients = rows_ref.shape[1]

    def clear(t, carry):
        for acc in accs:
            acc[pl.ds(pl.multiple_of(t * 64, 64), 64), :] = jnp.zeros((64, 128), jnp.float32)
        return carry

    lax.fori_loop(0, voxels // 64, clear, 0)
    copy.wait()
    base = block_ref[0] * q_count

    def step(t, carry):
        n = 0
        for q in range(q_count):
            for s in range(8):
                r = t * 8 + s
                i = index_smem[r, base + q]
                acc = accs[n % len(accs)]
                n += 1
                acc[pl.ds(i, 1), :] += rows_ref[q, pl.ds(r, 1), :]
        return carry

    lax.fori_loop(0, orients // 8, step, 0)

    def finish(t, carry):
        d = pl.ds(pl.multiple_of(t * 64, 64), 64)
        total = accs[0][d, :]
        for acc in accs[1:]:
            total = total + acc[d, :]
        out_ref[d, :] = total
        return carry

    lax.fori_loop(0, voxels // 64, finish, 0)


def scatter(rows, index, block, voxels):
    q_count = rows.shape[0]
    return pl.pallas_call(
        functools.partial(scatter_kernel, q_count),
        out_shape=jax.ShapeDtypeStruct((voxels, 128), jnp.float32),
        in_specs=[
            pl.BlockSpec(memory_space=pltpu.SMEM),
            pl.BlockSpec(memory_space=pltpu.VMEM),
            pl.BlockSpec(memory_space=pl.ANY),
        ],
        out_specs=pl.BlockSpec(memory_space=pltpu.VMEM),
        scratch_shapes=[pltpu.SMEM(index.shape, jnp.int32), pltpu.SemaphoreType.DMA]
        + [pltpu.VMEM((voxels, 128), jnp.float32)] * ACCS,
        compiler_params=pltpu.CompilerParams(vmem_limit_bytes=48 * 2**20),
    )(block, rows, index)


def local(counts, pixel_gain, slices, voxel_index, interp):
    frame_size = lax.axis_size("frame")
    orient_size = lax.axis_size("orient")
    me = lax.axis_index("frame")
    q_count = PART // 128
    voxels = VB_DEV * orient_size * frame_size
    rows = iterate(counts, pixel_gain, interp, slices)
    block = jnp.full((1,), me, jnp.int32)
    voxel_sum = scatter(rows, voxel_index, block, voxels)
    weight = lax.dynamic_slice_in_dim(interp, me * q_count, q_count, axis=1)
    targets = lax.dynamic_slice_in_dim(voxel_index, me * q_count, q_count, axis=1).reshape(1, -1)
    flat_weight = weight.reshape(1, -1)
    upper, lower = targets // VB_DEV, targets % VB_DEV
    slot = lax.broadcasted_iota(jnp.int32, (128, 1), 0)
    owner = 2 * (slot % 64) + slot // 64
    hot_upper = (upper == owner).astype(jnp.float32)
    hot_lower = jnp.where(lower == slot, flat_weight, 0.0)
    voxel_weight = lax.dot_general(
        hot_upper, hot_lower, (((1,), (1,)), ((), ())), precision=lax.Precision.HIGHEST
    )
    return reduce_blocks(
        voxel_sum.reshape(SIDE, SIDE, SIDE, 2, VB_DEV, 128), voxel_weight.reshape(2, SIDE, SIDE * SIDE, 128)
    )


def solution(mesh):
    placed = (
        P(("orient", "frame"), None),
        P(),
        P("orient", None),
        P("orient", None),
        P("orient", None),
    )
    return jax.shard_map(
        local, mesh=mesh, in_specs=placed, out_specs=P(("orient", "frame"), None), check_vma=False
    )
```

```python
import functools

import jax
import jax.numpy as jnp
from jax import lax
from jax.experimental import pallas as pl
from jax.experimental.pallas import tpu as pltpu
from jax.sharding import PartitionSpec as P

VB_DEV = 48
ACCS = 4


SIDE = 4
ORDERS = ((0, 1, 2), (1, 2, 0), (2, 0, 1))


def here():
    orient, frame = lax.axis_index("orient"), lax.axis_index("frame")
    return (orient // SIDE, orient % SIDE, frame // 2, frame % 2)


def device(place):
    x, y, z, core = place
    return (x * SIDE + y, z * 2 + core)


def moved(place, axis, step):
    out = list(place)
    out[axis] = (place[axis] + step) % SIDE
    return tuple(out)


def pick(ref, axis, value, ndim):
    return ref.at[tuple(value if a == axis else slice(None) for a in range(ndim))]


def sums_kernel(v_ref, w_ref, o_ref, pair_out, pair_in, s1, s1b, in1, s2, s2b, in2, s3, s3b, in3,
                wsum, wpair_in, win1, w2, win2, w3, win3,
                pair_sem, sem1, sem2, sem3, wpair_sem, wsem1, wsem2, wsem3):
    me = here()
    core = me[3]
    sibling = (me[0], me[1], me[2], 1 - core)
    barrier = pltpu.get_barrier_semaphore()
    peers = [sibling] + [moved(me, a, d) for a in range(3) for d in (1, 2, 3)]
    for peer in peers:
        pl.semaphore_signal(barrier, inc=1, device_id=device(peer), device_id_type=pl.DeviceIdType.MESH)
    for p in range(3):
        pair_out[p] = v_ref[:, :, :, 1 - core, 16 * p:16 * p + 16, :].astype(jnp.bfloat16)
    pl.semaphore_wait(barrier, len(peers))

    def send(src, dst, sems, slot, place):
        copy = pltpu.make_async_remote_copy(
            src_ref=src, dst_ref=dst, send_sem=sems.at[0, slot], recv_sem=sems.at[1, slot],
            device_id=device(place), device_id_type=pl.DeviceIdType.MESH)
        copy.start()
        return copy

    pair = [send(pair_out.at[p], pair_in.at[p], pair_sem, p, sibling) for p in range(3)]
    wpair = send(w_ref.at[1 - core], wpair_in, wpair_sem, 0, sibling)
    first, second, third = [], [], []
    for p in range(3):
        axis = ORDERS[p][0]
        pair[p].wait_recv()
        total = v_ref[:, :, :, core, 16 * p:16 * p + 16, :] + pair_in[p].astype(jnp.float32)
        s1[p] = total
        s1b[p] = total.astype(jnp.bfloat16)
        first.append([send(pick(s1b.at[p], axis, (me[axis] + d) % SIDE, 3), in1.at[p, d - 1], sem1, 3 * p + d - 1,
                           moved(me, axis, d)) for d in (1, 2, 3)])
    wpair.wait_recv()
    wsum[...] = w_ref[core] + wpair_in[...]
    wfirst = [send(wsum.at[(me[0] + d) % SIDE], win1.at[d - 1], wsem1, d - 1, moved(me, 0, d)) for d in (1, 2, 3)]
    for p in range(3):
        axis, nxt = ORDERS[p][0], ORDERS[p][1]
        for copy in first[p]:
            copy.wait_recv()
        own = pick(s1.at[p], axis, me[axis], 3)[...]
        total = own + in1[p, 0].astype(jnp.float32) + in1[p, 1].astype(jnp.float32) + in1[p, 2].astype(jnp.float32)
        s2[p] = total
        s2b[p] = total.astype(jnp.bfloat16)
        dim = nxt - (1 if nxt > axis else 0)
        second.append([send(pick(s2b.at[p], dim, (me[nxt] + d) % SIDE, 2), in2.at[p, d - 1], sem2, 3 * p + d - 1,
                            moved(me, nxt, d)) for d in (1, 2, 3)])
    for copy in wfirst:
        copy.wait_recv()
    w2[...] = wsum[me[0]] + win1[0] + win1[1] + win1[2]
    wsecond = [send(w2, win2.at[d - 1], wsem2, d - 1, moved(me, 1, d)) for d in (1, 2, 3)]
    for p in range(3):
        axis, nxt, last = ORDERS[p]
        for copy in second[p]:
            copy.wait_recv()
        dim = nxt - (1 if nxt > axis else 0)
        own = pick(s2.at[p], dim, me[nxt], 2)[...]
        total = own + in2[p, 0].astype(jnp.float32) + in2[p, 1].astype(jnp.float32) + in2[p, 2].astype(jnp.float32)
        s3[p] = total
        s3b[p] = total.astype(jnp.bfloat16)
        third.append([send(s3b.at[p, (me[last] + d) % SIDE], in3.at[p, d - 1], sem3, 3 * p + d - 1,
                           moved(me, last, d)) for d in (1, 2, 3)])
    for copy in wsecond:
        copy.wait_recv()
    w3[...] = w2[...] + win2[0] + win2[1] + win2[2]
    wthird = [send(w3, win3.at[d - 1], wsem3, d - 1, moved(me, 2, d)) for d in (1, 2, 3)]
    for copy in wthird:
        copy.wait_recv()
    weights = w3[...] + win3[0] + win3[1] + win3[2]
    mine = lax.broadcasted_iota(jnp.int32, weights.shape, 0) == me[1] * SIDE + me[2]
    row = jnp.sum(jnp.where(mine, weights, 0.0), axis=0, keepdims=True)
    shape = (o_ref.shape[0], 128)
    diagonal = lax.broadcasted_iota(jnp.int32, shape, 0) == lax.broadcasted_iota(jnp.int32, shape, 1)
    column = jnp.sum(jnp.where(diagonal, row, 0.0), axis=1, keepdims=True)
    scale = 1.0 / (1.0 + column)
    for p in range(3):
        for copy in third[p]:
            copy.wait_recv()
        own = s3[p, me[ORDERS[p][2]]]
        total = own + in3[p, 0].astype(jnp.float32) + in3[p, 1].astype(jnp.float32) + in3[p, 2].astype(jnp.float32)
        o_ref[16 * p:16 * p + 16, :] = total * scale[16 * p:16 * p + 16]
    for copies in pair, [wpair], *first, *second, *third, wfirst, wsecond, wthird:
        for copy in copies:
            copy.wait_send()


def reduce_blocks(voxel_sum, voxel_weight):
    f32, b16 = jnp.float32, jnp.bfloat16
    vm, dma = pltpu.VMEM, pltpu.SemaphoreType.DMA
    scratch = [
        vm((3, 4, 4, 4, 16, 128), b16), vm((3, 4, 4, 4, 16, 128), b16),
        vm((3, 4, 4, 4, 16, 128), f32), vm((3, 4, 4, 4, 16, 128), b16), vm((3, 3, 4, 4, 16, 128), b16),
        vm((3, 4, 4, 16, 128), f32), vm((3, 4, 4, 16, 128), b16), vm((3, 3, 4, 16, 128), b16),
        vm((3, 4, 16, 128), f32), vm((3, 4, 16, 128), b16), vm((3, 3, 16, 128), b16),
        vm((4, 16, 128), f32), vm((4, 16, 128), f32), vm((3, 16, 128), f32),
        vm((16, 128), f32), vm((3, 16, 128), f32), vm((16, 128), f32), vm((3, 16, 128), f32),
        dma((2, 3)), dma((2, 9)), dma((2, 9)), dma((2, 9)), dma((2, 1)), dma((2, 3)), dma((2, 3)), dma((2, 3)),
    ]
    vspec = pl.BlockSpec(memory_space=pltpu.VMEM)
    return pl.pallas_call(
        sums_kernel,
        out_shape=jax.ShapeDtypeStruct((48, 128), f32),
        in_specs=[vspec, vspec], out_specs=vspec, scratch_shapes=scratch,
        compiler_params=pltpu.CompilerParams(collective_id=3, has_side_effects=True, vmem_limit_bytes=40 * 2**20),
    )(voxel_sum, voxel_weight)


PARTS = 8
PART = 2048
HALF = 256
HELD = 272
CUT = 136
score_beta = 1.5
NT = (((1,), (1,)), ((), ()))


def iterate_kernel(counts_hbm, gain_ref, interp_ref, index_ref, slices_hbm, rows_hbm, voxel_weight_ref,
                   counts_ref, rows_ref, index_rows, weight_rows,
                   own, frames, part, stream, logs, log_mean, scores, pair_in, blocks_a, blocks_b, z1a_in, z1b_in, kept_a, kept_b, z2a_in, z2b_in,
                   shifted, photon, stat, stat2, stat3, sib_in, x_in, y_in, prob, gathered, mass,
                   load_sem, rows_sem, a2a_send, a2a_recv, g_send, g_recv, pair_sem, z1a_sem, z1b_sem, z2a_sem, z2b_sem, sib_sem,
                   x_send, x_recv, y_send, y_recv, ag_send, ag_recv, agc_sem):
    f32, b16 = jnp.float32, jnp.bfloat16
    x, y, z, core = me = here()
    plane = z * 2 + core
    pixel_count = PARTS * PART
    sibling = (x, y, z, 1 - core)
    near = (x, y, z + 1 - 2 * (z % 2), core)
    far = (x, y, 3 - z, core)
    group = ((z + 1) // 2) % 2
    spot = z // 2
    xl, xr, yl, yr = (x + 3) % 4, (x + 1) % 4, (y + 3) % 4, (y + 1) % 4
    to_xr, to_xl = (xr, y, z, core), (xl, y, z, core)
    to_yr, to_yl = (x, yr, z, core), (x, yl, z, core)

    def remote(src, dst, send_sem, recv_sem, place):
        return pltpu.make_async_remote_copy(
            src_ref=src, dst_ref=dst, send_sem=send_sem, recv_sem=recv_sem,
            device_id=device(place), device_id_type=pl.DeviceIdType.MESH)

    def when(s, body, limit=PARTS):
        pl.when((s >= 0) & (s < limit))(lambda: body(s))

    count_copy = pltpu.make_async_copy(counts_hbm, counts_ref, load_sem.at[3])
    count_copy.start()
    load = pltpu.make_async_copy(
        slices_hbm.at[:, pl.ds(pl.multiple_of(plane * PART, PART), PART)], part, load_sem.at[0])
    load.start()

    def stream_copy(j):
        return pltpu.make_async_copy(
            slices_hbm.at[pl.ds(pl.multiple_of(core * HALF, HALF), HALF), pl.ds(pl.multiple_of(j * PART, PART), PART)],
            stream.at[j % 2], load_sem.at[1 + j % 2])

    stream_copy(0).start()
    stream_copy(1).start()

    barrier = pltpu.get_barrier_semaphore()
    column = [(plane + d) % PARTS for d in range(1, PARTS)]
    peers = [(x, y, k // 2, k % 2) for k in column]
    peers += [moved(me, 0, d) for d in (1, 2, 3)] + [moved(me, 1, d) for d in (1, 2, 3)]
    for peer in peers:
        pl.semaphore_signal(barrier, inc=1, device_id=device(peer), device_id_type=pl.DeviceIdType.MESH)

    def correct(j, carry):
        lanes = pl.ds(pl.multiple_of(j * PART, PART), PART)
        own[j] = (counts_ref[:, lanes].astype(f32) * gain_ref[:, lanes]).astype(b16)
        return carry

    count_copy.wait()
    lax.fori_loop(0, PARTS, correct, 0)
    frames[plane, x, y] = own[plane]
    pl.semaphore_wait(barrier, len(peers))

    def a2a_copy(d):
        k = (plane + d) % PARTS
        return remote(own.at[k], frames.at[plane, x, y], a2a_send.at[d - 1], a2a_recv.at[plane], (x, y, k // 2, k % 2))

    def a2a_start(d, carry):
        a2a_copy(d).start()
        return carry

    lax.fori_loop(1, PARTS, a2a_start, 0)

    def order(i):
        return jnp.where(i == 0, plane, jnp.where(i - 1 < plane, i - 1, i))

    def gather_copy(i, n):
        s = order(i)
        lo, hi = pl.ds(0, 16), pl.ds(16, 16)
        left, right = pl.ds(0, PART // 2), pl.ds(PART // 2, PART // 2)
        two, other = pl.ds(0, 2), pl.ds(2, 2)
        every = pl.ds(0, 4)
        full = pl.ds(0, PART)
        where, place = [
            ((s, x, y, lo, full), to_xr), ((s, x, y, lo, full), to_xl),
            ((s, x, y, hi, full), to_yr), ((s, x, y, hi, full), to_yl),
            ((s, xl, y, lo, left), to_xr), ((s, xr, y, lo, right), to_xl),
            ((s, x, yl, hi, left), to_yr), ((s, x, yr, hi, right), to_yl),
            ((s, every, y, lo, full), to_yr), ((s, every, y, lo, full), to_yl),
            ((s, x, every, hi, full), to_xr), ((s, x, every, hi, full), to_xl),
            ((s, two, yl, lo, full), to_yr), ((s, other, yr, lo, full), to_yl),
            ((s, xl, two, hi, full), to_xr), ((s, xr, other, hi, full), to_xl),
        ][n]
        return remote(frames.at[where], frames.at[where], g_send.at[i, n], g_recv.at[i, n], place)

    def gather(stage):
        def body(i):
            if stage == 1:
                s = order(i)

                @pl.when(s != plane)
                def _():
                    remote(own.at[0], frames.at[s, x, y], a2a_send.at[0], a2a_recv.at[s], sibling).wait_recv()
            else:
                for n in range(4 * stage - 8, 4 * stage - 4):
                    gather_copy(i, n).wait_recv()
            if stage < 5:
                for n in range(4 * stage - 4, 4 * stage):
                    gather_copy(i, n).start()
        return body

    when(0, gather(1))

    log_mean[...] = jnp.zeros_like(log_mean)

    def add_means(j, carry):
        stream_copy(j).wait()
        log_mean[...] += jnp.dot(stream[j % 2], jnp.ones((PART, 128), b16), preferred_element_type=f32)

        @pl.when(j + 2 < PARTS)
        def _():
            stream_copy(j + 2).start()
        return carry

    lax.fori_loop(0, PARTS, add_means, 0)
    log_mean[...] = jnp.log(log_mean[...] / pixel_count)
    gather(2)(0)
    load.wait()

    def take_logs(h):
        def body(j, carry):
            rows = pl.ds(pl.multiple_of(j * 16, 16), 16)
            logs[h, rows, :] = jnp.log(part[pl.ds(pl.multiple_of(h * HALF + j * 16, 16), 16), :].astype(f32)).astype(b16)
            return carry
        lax.fori_loop(0, HALF // 16, body, 0)
        logs[h, HALF:HELD, :] = jnp.ones((HELD - HALF, PART), b16)

    take_logs(0)
    gather(3)(0)
    gather(1)(1)
    take_logs(1)
    gather(2)(1)
    gather(1)(2)
    weight = interp_ref[...]
    weight_hi = weight.astype(b16)
    weight_lo = (weight - weight_hi.astype(f32)).astype(b16)

    def spread(j, carry):
        lane = lax.broadcasted_iota(jnp.int32, (128, 256), 0)
        column_of = plane * 16 + 2 * j + lax.broadcasted_iota(jnp.int32, (128, 256), 1) // 128
        hot = jnp.where(lane == column_of, 1.0, 0.0).astype(b16)
        out = jnp.dot(weight_hi, hot, preferred_element_type=f32) + jnp.dot(weight_lo, hot, preferred_element_type=f32)
        rows_ref[2 * j] = out[:, :128]
        rows_ref[2 * j + 1] = out[:, 128:]
        return carry

    lax.fori_loop(0, PARTS, spread, 0)
    mass[...] = jnp.zeros_like(mass)
    voxel_weight_ref[...] = jnp.zeros_like(voxel_weight_ref)
    index_rows[...] = index_ref[...].astype(f32).T
    weight_rows[...] = weight.T
    first_q = pl.ds(pl.multiple_of(plane * 16, 16), 16)
    index_part, weight_part = index_rows[first_q, :], weight_rows[first_q, :]
    for q in range(16):
        index_rows[8 * q:8 * q + 8] = jnp.broadcast_to(index_part[q:q + 1], (8, 2 * HALF))
        weight_rows[8 * q:8 * q + 8] = jnp.broadcast_to(weight_part[q:q + 1], (8, 2 * HALF))

    def clear(j, carry):
        some = pl.ds(pl.multiple_of(j * 16, 16), 16)
        gathered[some, :] = 0.25 * part[some, :].astype(f32)
        return carry

    lax.fori_loop(0, 2 * HALF // 16, clear, 0)

    def pair_copy(s):
        return remote(scores.at[s % 2, 1 - core], pair_in.at[s], pair_sem.at[0, s], pair_sem.at[1, s], sibling)

    def z1_copies(s):
        return (remote(blocks_a.at[s % 2, 1 - group], z1a_in.at[s], z1a_sem.at[0, s], z1a_sem.at[1, s], near),
                remote(blocks_b.at[s % 2, 1 - spot], z1b_in.at[s], z1b_sem.at[0, s], z1b_sem.at[1, s], far))

    def z2_copies(s):
        return (remote(kept_a.at[s % 2, 1 - spot], z2a_in.at[s], z2a_sem.at[0, s], z2a_sem.at[1, s], far),
                remote(kept_b.at[s % 2, 1 - z % 2], z2b_in.at[s], z2b_sem.at[0, s], z2b_sem.at[1, s], near))

    def sib_copy(s):
        return remote(stat.at[s % 2], sib_in.at[s], sib_sem.at[0, s], sib_sem.at[1, s], sibling)

    def x_copy(s, d):
        return remote(stat2.at[s % 2], x_in.at[s, d - 1], x_send.at[s, d - 1], x_recv.at[s, d - 1], moved(me, 0, d))

    def y_copy(s, d):
        return remote(stat3.at[s % 2], y_in.at[s, d - 1], y_send.at[s, d - 1], y_recv.at[s, d - 1], moved(me, 1, d))

    def ag_copies(s):
        lanes = pl.ds(pl.multiple_of(z * 128, 128), 128)
        return [remote(prob.at[s, core, :, lanes], prob.at[s, core, :, lanes], ag_send.at[s, d - 1], ag_recv.at[s, d - 1],
                       moved(me, 2, d)) for d in (1, 2, 3)]

    def agc_copy(s):
        return remote(prob.at[s, core], prob.at[s, core], agc_sem.at[0, s], agc_sem.at[1, s], sibling)

    def multiply(s):
        pl.when(s >= 2)(lambda: pair_copy(s - 2).wait_send())

        def tile(j, carry):
            block = frames[s, pl.ds(2 * j, 2)].reshape(HALF, PART)
            lanes = pl.ds(pl.multiple_of(j * HALF, HALF), HALF)
            for h in range(2):
                scores[s % 2, h, :, lanes] = lax.dot_general(logs[h], block, NT, preferred_element_type=f32)
            return carry

        lax.fori_loop(0, 2, tile, 0)
        pair_copy(s).start()

    def settle(copies):
        for copy in copies:
            copy.wait_send()

    def add_pair(s):
        pl.when(s >= 2)(lambda: settle(z1_copies(s - 2)))
        pair_copy(s).wait_recv()
        for b, (g, n) in enumerate(((0, 0), (1, 0), (1, 1), (0, 1))):
            lanes = slice(128 * b, 128 * b + 128)
            total = scores[s % 2, core, :, lanes] + pair_in[s, :, lanes]
            blocks_a[s % 2, g, n] = total[:CUT]
            blocks_b[s % 2, b // 2, b % 2] = total[CUT:]
        for copy in z1_copies(s):
            copy.start()

    def add_first(s):
        pl.when(s >= 2)(lambda: settle(z2_copies(s - 2)))
        for copy in z1_copies(s):
            copy.wait_recv()
        kept_a[s % 2] = blocks_a[s % 2, group] + z1a_in[s]
        kept_b[s % 2] = blocks_b[s % 2, spot] + z1b_in[s]
        for copy in z2_copies(s):
            copy.start()

    first_row = lax.broadcasted_iota(jnp.int32, (8, 128), 0) == 0

    def combine(tiles):
        peak = tiles[0][0:1]
        for tile in tiles[1:]:
            peak = jnp.maximum(peak, tile[0:1])
        total = sum(tile[1:2] * jnp.exp(tile[0:1] - peak) for tile in tiles)
        return peak, total

    def score(s):
        pl.when(s >= 2)(lambda: sib_copy(s - 2).wait_send())
        for copy in z2_copies(s):
            copy.wait_recv()
        upper = kept_a[s % 2, spot] + z2a_in[s]
        lower = kept_b[s % 2, z % 2] + z2b_in[s]
        photons = lower[HALF - CUT:HALF - CUT + 1]
        value = jnp.concatenate([upper, lower[:HALF - CUT]], axis=0)
        value = (value - photons * log_mean[...]) * (score_beta / pixel_count)
        peak = jnp.max(value, axis=0, keepdims=True)
        value = jnp.exp(value - peak)
        shifted[s % 2] = value
        photon[s % 2] = jnp.broadcast_to(photons, (8, 128))
        stat[s % 2] = jnp.where(first_row, peak, jnp.sum(value, axis=0, keepdims=True))
        sib_copy(s).start()

    def add_sibling(s):
        pl.when(s >= 2)(lambda: settle([x_copy(s - 2, d) for d in (1, 2, 3)]))
        sib_copy(s).wait_recv()
        peak, total = combine([stat[s % 2], sib_in[s]])
        stat2[s % 2] = jnp.where(first_row, peak, total)
        for d in (1, 2, 3):
            x_copy(s, d).start()

    def add_x(s):
        pl.when(s >= 2)(lambda: settle([y_copy(s - 2, d) for d in (1, 2, 3)]))
        for d in (1, 2, 3):
            x_copy(s, d).wait_recv()
        peak, total = combine([stat2[s % 2], x_in[s, 0], x_in[s, 1], x_in[s, 2]])
        stat3[s % 2] = jnp.where(first_row, peak, total)
        for d in (1, 2, 3):
            y_copy(s, d).start()

    def normalise(s):
        for d in (1, 2, 3):
            y_copy(s, d).wait_recv()
        peak, total = combine([stat3[s % 2], y_in[s, 0], y_in[s, 1], y_in[s, 2]])
        factor = jnp.exp(stat[s % 2][0:1] - peak) / total
        lanes = pl.ds(pl.multiple_of(z * 128, 128), 128)
        prob[s, core, :HALF, lanes] = (shifted[s % 2] * factor).astype(b16)
        photons = photon[s % 2][0:1]
        upper = photons.astype(b16).astype(f32)
        row = lax.broadcasted_iota(jnp.int32, (HELD - HALF, 128), 0)
        prob[s, core, HALF:, lanes] = jnp.where(row == 0, upper, jnp.where(row == 1, photons - upper, 0.0)).astype(b16)
        for copy in ag_copies(s):
            copy.start()

    def share_pair(s):
        for copy in ag_copies(s):
            copy.wait_recv()
        agc_copy(s).start()

    def gather_pixels(s):
        agc_copy(s).wait_recv()
        for h in range(2):
            mass[h] += lax.dot_general(prob[s, h, :HALF], prob[s, 0, HALF:], NT, preferred_element_type=f32)

        def tile(j, carry):
            lanes = pl.ds(pl.multiple_of(j * 256, 256), 256)
            block = frames[s, :, :, :, lanes].reshape(2 * HALF, 256)
            for h in range(2):
                gathered[h * HALF:h * HALF + HALF, lanes] += jnp.dot(prob[s, h, :HALF], block, preferred_element_type=f32)
            return carry

        lax.fori_loop(0, PARTS, tile, 0)

    def weigh(t):
        for q in (2 * t, 2 * t + 1):
            rows = pl.ds(pl.multiple_of(q * 8, 8), 8)
            target = index_rows[rows, :][0:1].astype(jnp.int32)
            amount = weight_rows[rows, :][0:1]
            owner = (target * 43691) >> 21
            lower = target - 48 * owner
            slot = (owner & 1) * 64 + (owner >> 1)
            row = lax.broadcasted_iota(jnp.int32, (128, 2 * HALF), 0)
            amount_hi = amount.astype(b16).astype(f32)
            hot = jnp.where(row == slot, 1.0, 0.0).astype(b16)
            parts = jnp.concatenate([jnp.where(row == lower, amount_hi, 0.0).astype(b16),
                                     jnp.where(row == lower, amount - amount_hi, 0.0).astype(b16)], axis=0)
            out = lax.dot_general(hot, parts, NT, preferred_element_type=f32)
            voxel_weight_ref[...] += out[:, :128] + out[:, 128:]

    def tick(t, carry):
        when(t + 2, gather(3))
        when(t + 3, gather(2))
        when(t + 4, gather(1))
        when(t + 1, gather(4))
        when(t - 2, add_pair)
        when(t - 3, score)
        when(t - 4, add_x)
        when(t - 5, share_pair)
        when(t, weigh)
        when(t, gather(5))
        when(t - 1, multiply)
        when(t - 2, add_first)
        when(t - 3, add_sibling)
        when(t - 4, normalise)
        when(t - 5, gather_pixels)
        return carry

    lax.fori_loop(-1, PARTS + 5, tick, 0)

    share = 1.0 / (jnp.sum(mass[...], axis=2, keepdims=True) * (1.0 / pixel_count) + 0.25)
    writes = []
    for q in range(PART // 128):
        for h in range(2):
            lanes, some = slice(128 * q, 128 * q + 128), slice(h * HALF, h * HALF + HALF)
            rows_ref[q, some] = rows_ref[q, some] * (gathered[some, lanes] * share[h])
        writes.append(pltpu.make_async_copy(rows_ref.at[q], rows_hbm.at[q], rows_sem.at[q]))
        writes[-1].start()

    def drain(i, carry):
        for n in range(16):
            gather_copy(i, n).wait_send()
        settle(ag_copies(i))
        agc_copy(i).wait_send()
        return carry

    lax.fori_loop(0, PARTS, drain, 0)

    def drain_a2a(d, carry):
        a2a_copy(d).wait_send()
        return carry

    lax.fori_loop(1, PARTS, drain_a2a, 0)
    for s in (PARTS - 2, PARTS - 1):
        pair_copy(s).wait_send()
        settle(z1_copies(s))
        settle(z2_copies(s))
        sib_copy(s).wait_send()
        for d in (1, 2, 3):
            x_copy(s, d).wait_send()
            y_copy(s, d).wait_send()
    for write in writes:
        write.wait()


def iterate(counts, gain, interp, index, slices):
    f32, b16 = jnp.float32, jnp.bfloat16
    vm, dma = pltpu.VMEM, pltpu.SemaphoreType.DMA
    n = PARTS
    scratch = [
        vm((32, n * PART), jnp.int32), vm((PART // 128, 2 * HALF, 128), f32), vm((128, 2 * HALF), f32), vm((128, 2 * HALF), f32),
        vm((n, 32, PART), b16), vm((n, 4, 4, 32, PART), b16), vm((2 * HALF, PART), b16), vm((2, HALF, PART), b16),
        vm((2, HELD, PART), b16), vm((HALF, 128), f32), vm((2, 2, HELD, 512), f32), vm((n, HELD, 512), f32),
        vm((2, 2, 2, CUT, 128), f32), vm((2, 2, 2, CUT, 128), f32), vm((n, 2, CUT, 128), f32), vm((n, 2, CUT, 128), f32),
        vm((2, 2, CUT, 128), f32), vm((2, 2, CUT, 128), f32), vm((n, CUT, 128), f32), vm((n, CUT, 128), f32),
        vm((2, HALF, 128), f32), vm((2, 8, 128), f32), vm((2, 8, 128), f32), vm((2, 8, 128), f32), vm((2, 8, 128), f32),
        vm((n, 8, 128), f32), vm((n, 3, 8, 128), f32), vm((n, 3, 8, 128), f32),
        vm((n, 2, HELD, 512), b16), vm((2 * HALF, PART), f32), vm((2, HALF, HELD - HALF), f32),
        dma((4,)), dma((PART // 128,)), dma((n - 1,)), dma((n,)), dma((n, 16)), dma((n, 16)),
        dma((2, n)), dma((2, n)), dma((2, n)), dma((2, n)), dma((2, n)), dma((2, n)),
        dma((n, 3)), dma((n, 3)), dma((n, 3)), dma((n, 3)), dma((n, 3)), dma((n, 3)), dma((2, n)),
    ]
    vspec, anyspec = pl.BlockSpec(memory_space=pltpu.VMEM), pl.BlockSpec(memory_space=pl.ANY)
    return pl.pallas_call(
        iterate_kernel,
        out_shape=[jax.ShapeDtypeStruct((PART // 128, 2 * HALF, 128), f32), jax.ShapeDtypeStruct((128, 128), f32)],
        in_specs=[anyspec, vspec, vspec, vspec, anyspec], out_specs=[anyspec, vspec], scratch_shapes=scratch,
        compiler_params=pltpu.CompilerParams(collective_id=2, has_side_effects=True, vmem_limit_bytes=62 * 2**20),
    )(counts, gain.reshape(1, -1), interp, index, slices)


def scatter_kernel(q_count, rows_ref, index_hbm, out_ref, index_smem, sem, *accs):
    copy = pltpu.make_async_copy(index_hbm, index_smem, sem)
    copy.start()
    voxels = out_ref.shape[0]
    orients = rows_ref.shape[1]

    def clear(t, carry):
        for acc in accs:
            acc[pl.ds(pl.multiple_of(t * 64, 64), 64), :] = jnp.zeros((64, 128), jnp.float32)
        return carry

    lax.fori_loop(0, voxels // 64, clear, 0)
    copy.wait()
    base = lax.axis_index("frame") * q_count

    def step(t, carry):
        n = 0
        for q in range(q_count):
            for s in range(8):
                r = t * 8 + s
                i = index_smem[r, base + q]
                acc = accs[n % len(accs)]
                n += 1
                acc[pl.ds(i, 1), :] += rows_ref[q, pl.ds(r, 1), :]
        return carry

    lax.fori_loop(0, orients // 8, step, 0)

    def finish(t, carry):
        d = pl.ds(pl.multiple_of(t * 64, 64), 64)
        total = accs[0][d, :]
        for acc in accs[1:]:
            total = total + acc[d, :]
        out_ref[d, :] = total
        return carry

    lax.fori_loop(0, voxels // 64, finish, 0)


def scatter(rows, index, voxels):
    q_count = rows.shape[0]
    return pl.pallas_call(
        functools.partial(scatter_kernel, q_count),
        out_shape=jax.ShapeDtypeStruct((voxels, 128), jnp.float32),
        in_specs=[
            pl.BlockSpec(memory_space=pltpu.VMEM),
            pl.BlockSpec(memory_space=pl.ANY),
        ],
        out_specs=pl.BlockSpec(memory_space=pltpu.VMEM),
        scratch_shapes=[pltpu.SMEM(index.shape, jnp.int32), pltpu.SemaphoreType.DMA]
        + [pltpu.VMEM((voxels, 128), jnp.float32)] * ACCS,
        compiler_params=pltpu.CompilerParams(vmem_limit_bytes=48 * 2**20),
    )(rows, index)


def local(counts, pixel_gain, slices, voxel_index, interp):
    voxels = VB_DEV * lax.axis_size("orient") * lax.axis_size("frame")
    rows, voxel_weight = iterate(counts, pixel_gain, interp, voxel_index, slices)
    voxel_sum = scatter(rows, voxel_index, voxels)
    return reduce_blocks(
        voxel_sum.reshape(SIDE, SIDE, SIDE, 2, VB_DEV, 128), voxel_weight.reshape(2, SIDE, SIDE * SIDE, 128)
    )


def solution(mesh):
    placed = (
        P(("orient", "frame"), None),
        P(),
        P("orient", None),
        P("orient", None),
        P("orient", None),
    )
    return jax.shard_map(
        local, mesh=mesh, in_specs=placed, out_specs=P(("orient", "frame"), None), check_vma=False
    )
```

```python
import functools

import jax
import jax.numpy as jnp
from jax import lax
from jax.experimental import pallas as pl
from jax.experimental.pallas import tpu as pltpu
from jax.sharding import PartitionSpec as P

VB_DEV = 48
ACCS = 4


SIDE = 4
ORDERS = ((0, 1, 2), (1, 2, 0), (2, 0, 1))


def here():
    orient, frame = lax.axis_index("orient"), lax.axis_index("frame")
    return (orient // SIDE, orient % SIDE, frame // 2, frame % 2)


def device(place):
    x, y, z, core = place
    return (x * SIDE + y, z * 2 + core)


def moved(place, axis, step):
    out = list(place)
    out[axis] = (place[axis] + step) % SIDE
    return tuple(out)


def pick(ref, axis, value, ndim):
    return ref.at[tuple(value if a == axis else slice(None) for a in range(ndim))]


def sums_kernel(v_ref, w_ref, o_ref, pair_out, pair_in, s1, s1b, in1, s2, s2b, in2, s3, s3b, in3,
                wsum, wpair_in, win1, w2, win2, w3, win3,
                pair_sem, sem1, sem2, sem3, wpair_sem, wsem1, wsem2, wsem3):
    me = here()
    core = me[3]
    sibling = (me[0], me[1], me[2], 1 - core)
    barrier = pltpu.get_barrier_semaphore()
    peers = [sibling] + [moved(me, a, d) for a in range(3) for d in (1, 2, 3)]
    for peer in peers:
        pl.semaphore_signal(barrier, inc=1, device_id=device(peer), device_id_type=pl.DeviceIdType.MESH)
    for p in range(3):
        pair_out[p] = v_ref[:, :, :, 1 - core, 16 * p:16 * p + 16, :].astype(jnp.bfloat16)
    pl.semaphore_wait(barrier, len(peers))

    def send(src, dst, sems, slot, place):
        copy = pltpu.make_async_remote_copy(
            src_ref=src, dst_ref=dst, send_sem=sems.at[0, slot], recv_sem=sems.at[1, slot],
            device_id=device(place), device_id_type=pl.DeviceIdType.MESH)
        copy.start()
        return copy

    pair = [send(pair_out.at[p], pair_in.at[p], pair_sem, p, sibling) for p in range(3)]
    wpair = send(w_ref.at[1 - core], wpair_in, wpair_sem, 0, sibling)
    first, second, third = [], [], []
    for p in range(3):
        axis = ORDERS[p][0]
        pair[p].wait_recv()
        total = v_ref[:, :, :, core, 16 * p:16 * p + 16, :] + pair_in[p].astype(jnp.float32)
        s1[p] = total
        s1b[p] = total.astype(jnp.bfloat16)
        first.append([send(pick(s1b.at[p], axis, (me[axis] + d) % SIDE, 3), in1.at[p, d - 1], sem1, 3 * p + d - 1,
                           moved(me, axis, d)) for d in (1, 2, 3)])
    wpair.wait_recv()
    wsum[...] = w_ref[core] + wpair_in[...]
    wfirst = [send(wsum.at[(me[0] + d) % SIDE], win1.at[d - 1], wsem1, d - 1, moved(me, 0, d)) for d in (1, 2, 3)]
    for p in range(3):
        axis, nxt = ORDERS[p][0], ORDERS[p][1]
        for copy in first[p]:
            copy.wait_recv()
        own = pick(s1.at[p], axis, me[axis], 3)[...]
        total = own + in1[p, 0].astype(jnp.float32) + in1[p, 1].astype(jnp.float32) + in1[p, 2].astype(jnp.float32)
        s2[p] = total
        s2b[p] = total.astype(jnp.bfloat16)
        dim = nxt - (1 if nxt > axis else 0)
        second.append([send(pick(s2b.at[p], dim, (me[nxt] + d) % SIDE, 2), in2.at[p, d - 1], sem2, 3 * p + d - 1,
                            moved(me, nxt, d)) for d in (1, 2, 3)])
    for copy in wfirst:
        copy.wait_recv()
    w2[...] = wsum[me[0]] + win1[0] + win1[1] + win1[2]
    wsecond = [send(w2, win2.at[d - 1], wsem2, d - 1, moved(me, 1, d)) for d in (1, 2, 3)]
    for p in range(3):
        axis, nxt, last = ORDERS[p]
        for copy in second[p]:
            copy.wait_recv()
        dim = nxt - (1 if nxt > axis else 0)
        own = pick(s2.at[p], dim, me[nxt], 2)[...]
        total = own + in2[p, 0].astype(jnp.float32) + in2[p, 1].astype(jnp.float32) + in2[p, 2].astype(jnp.float32)
        s3[p] = total
        s3b[p] = total.astype(jnp.bfloat16)
        third.append([send(s3b.at[p, (me[last] + d) % SIDE], in3.at[p, d - 1], sem3, 3 * p + d - 1,
                           moved(me, last, d)) for d in (1, 2, 3)])
    for copy in wsecond:
        copy.wait_recv()
    w3[...] = w2[...] + win2[0] + win2[1] + win2[2]
    wthird = [send(w3, win3.at[d - 1], wsem3, d - 1, moved(me, 2, d)) for d in (1, 2, 3)]
    for copy in wthird:
        copy.wait_recv()
    weights = w3[...] + win3[0] + win3[1] + win3[2]
    mine = lax.broadcasted_iota(jnp.int32, weights.shape, 0) == me[1] * SIDE + me[2]
    row = jnp.sum(jnp.where(mine, weights, 0.0), axis=0, keepdims=True)
    shape = (o_ref.shape[0], 128)
    diagonal = lax.broadcasted_iota(jnp.int32, shape, 0) == lax.broadcasted_iota(jnp.int32, shape, 1)
    column = jnp.sum(jnp.where(diagonal, row, 0.0), axis=1, keepdims=True)
    scale = 1.0 / (1.0 + column)
    for p in range(3):
        for copy in third[p]:
            copy.wait_recv()
        own = s3[p, me[ORDERS[p][2]]]
        total = own + in3[p, 0].astype(jnp.float32) + in3[p, 1].astype(jnp.float32) + in3[p, 2].astype(jnp.float32)
        o_ref[16 * p:16 * p + 16, :] = total * scale[16 * p:16 * p + 16]
    for copies in pair, [wpair], *first, *second, *third, wfirst, wsecond, wthird:
        for copy in copies:
            copy.wait_send()


def reduce_blocks(voxel_sum, voxel_weight):
    f32, b16 = jnp.float32, jnp.bfloat16
    vm, dma = pltpu.VMEM, pltpu.SemaphoreType.DMA
    scratch = [
        vm((3, 4, 4, 4, 16, 128), b16), vm((3, 4, 4, 4, 16, 128), b16),
        vm((3, 4, 4, 4, 16, 128), f32), vm((3, 4, 4, 4, 16, 128), b16), vm((3, 3, 4, 4, 16, 128), b16),
        vm((3, 4, 4, 16, 128), f32), vm((3, 4, 4, 16, 128), b16), vm((3, 3, 4, 16, 128), b16),
        vm((3, 4, 16, 128), f32), vm((3, 4, 16, 128), b16), vm((3, 3, 16, 128), b16),
        vm((4, 16, 128), f32), vm((4, 16, 128), f32), vm((3, 16, 128), f32),
        vm((16, 128), f32), vm((3, 16, 128), f32), vm((16, 128), f32), vm((3, 16, 128), f32),
        dma((2, 3)), dma((2, 9)), dma((2, 9)), dma((2, 9)), dma((2, 1)), dma((2, 3)), dma((2, 3)), dma((2, 3)),
    ]
    vspec = pl.BlockSpec(memory_space=pltpu.VMEM)
    return pl.pallas_call(
        sums_kernel,
        out_shape=jax.ShapeDtypeStruct((48, 128), f32),
        in_specs=[vspec, vspec], out_specs=vspec, scratch_shapes=scratch,
        compiler_params=pltpu.CompilerParams(collective_id=3, has_side_effects=True, vmem_limit_bytes=40 * 2**20),
    )(voxel_sum, voxel_weight)


PARTS = 8
PART = 2048
HALF = 256
HELD = 272
CUT = 136
score_beta = 1.5
NT = (((1,), (1,)), ((), ()))


def iterate_kernel(counts_hbm, gain_ref, interp_ref, index_ref, slices_hbm, rows_hbm, voxel_weight_ref,
                   counts_ref, rows_ref, index_rows, weight_rows,
                   own, frames, part, stream, logs, log_mean, scores, pair_in, blocks_a, blocks_b, z1a_in, z1b_in, kept_a, kept_b, z2a_in, z2b_in,
                   shifted, photon, stat, stat2, stat3, sib_in, x_in, y_in, prob, gathered, mass,
                   load_sem, rows_sem, a2a_send, a2a_recv, g_send, g_recv, pair_sem, z1a_sem, z1b_sem, z2a_sem, z2b_sem, sib_sem,
                   x_send, x_recv, y_send, y_recv, ag_send, ag_recv, agc_sem):
    f32, b16 = jnp.float32, jnp.bfloat16
    x, y, z, core = me = here()
    plane = z * 2 + core
    pixel_count = PARTS * PART
    sibling = (x, y, z, 1 - core)
    near = (x, y, z + 1 - 2 * (z % 2), core)
    far = (x, y, 3 - z, core)
    group = ((z + 1) // 2) % 2
    spot = z // 2
    xl, xr, yl, yr = (x + 3) % 4, (x + 1) % 4, (y + 3) % 4, (y + 1) % 4
    to_xr, to_xl = (xr, y, z, core), (xl, y, z, core)
    to_yr, to_yl = (x, yr, z, core), (x, yl, z, core)

    def remote(src, dst, send_sem, recv_sem, place):
        return pltpu.make_async_remote_copy(
            src_ref=src, dst_ref=dst, send_sem=send_sem, recv_sem=recv_sem,
            device_id=device(place), device_id_type=pl.DeviceIdType.MESH)

    def when(s, body, limit=PARTS):
        pl.when((s >= 0) & (s < limit))(lambda: body(s))

    count_copy = pltpu.make_async_copy(counts_hbm, counts_ref, load_sem.at[3])
    count_copy.start()
    load = pltpu.make_async_copy(
        slices_hbm.at[:, pl.ds(pl.multiple_of(plane * PART, PART), PART)], part, load_sem.at[0])
    load.start()

    def stream_copy(j):
        return pltpu.make_async_copy(
            slices_hbm.at[pl.ds(pl.multiple_of(core * HALF, HALF), HALF), pl.ds(pl.multiple_of(j * PART, PART), PART)],
            stream.at[j % 2], load_sem.at[1 + j % 2])

    stream_copy(0).start()
    stream_copy(1).start()

    barrier = pltpu.get_barrier_semaphore()
    column = [(plane + d) % PARTS for d in range(1, PARTS)]
    peers = [(x, y, k // 2, k % 2) for k in column]
    peers += [moved(me, 0, d) for d in (1, 2, 3)] + [moved(me, 1, d) for d in (1, 2, 3)]
    for peer in peers:
        pl.semaphore_signal(barrier, inc=1, device_id=device(peer), device_id_type=pl.DeviceIdType.MESH)

    def correct(j, carry):
        lanes = pl.ds(pl.multiple_of(j * PART, PART), PART)
        own[j] = (counts_ref[:, lanes].astype(f32) * gain_ref[:, lanes]).astype(b16)
        return carry

    count_copy.wait()
    lax.fori_loop(0, PARTS, correct, 0)
    frames[plane, x, y] = own[plane]
    pl.semaphore_wait(barrier, len(peers))

    def a2a_copy(d):
        k = (plane + d) % PARTS
        return remote(own.at[k], frames.at[plane, x, y], a2a_send.at[d - 1], a2a_recv.at[plane], (x, y, k // 2, k % 2))

    def a2a_start(d, carry):
        a2a_copy(d).start()
        return carry

    lax.fori_loop(1, PARTS, a2a_start, 0)

    def order(i):
        return jnp.where(i == 0, plane, jnp.where(i - 1 < plane, i - 1, i))

    def gather_copy(i, n):
        s = order(i)
        lo, hi = pl.ds(0, 16), pl.ds(16, 16)
        left, right = pl.ds(0, PART // 2), pl.ds(PART // 2, PART // 2)
        two, other = pl.ds(0, 2), pl.ds(2, 2)
        every = pl.ds(0, 4)
        full = pl.ds(0, PART)
        where, place = [
            ((s, x, y, lo, full), to_xr), ((s, x, y, lo, full), to_xl),
            ((s, x, y, hi, full), to_yr), ((s, x, y, hi, full), to_yl),
            ((s, xl, y, lo, left), to_xr), ((s, xr, y, lo, right), to_xl),
            ((s, x, yl, hi, left), to_yr), ((s, x, yr, hi, right), to_yl),
            ((s, every, y, lo, full), to_yr), ((s, every, y, lo, full), to_yl),
            ((s, x, every, hi, full), to_xr), ((s, x, every, hi, full), to_xl),
            ((s, two, yl, lo, full), to_yr), ((s, other, yr, lo, full), to_yl),
            ((s, xl, two, hi, full), to_xr), ((s, xr, other, hi, full), to_xl),
        ][n]
        return remote(frames.at[where], frames.at[where], g_send.at[i, n], g_recv.at[i, n], place)

    def gather(stage):
        def body(i):
            if stage == 1:
                s = order(i)

                @pl.when(s != plane)
                def _():
                    remote(own.at[0], frames.at[s, x, y], a2a_send.at[0], a2a_recv.at[s], sibling).wait_recv()
            else:
                for n in range(4 * stage - 8, 4 * stage - 4):
                    gather_copy(i, n).wait_recv()
            if stage < 5:
                for n in range(4 * stage - 4, 4 * stage):
                    gather_copy(i, n).start()
        return body

    when(0, gather(1))

    log_mean[...] = jnp.zeros_like(log_mean)

    def add_means(j, carry):
        stream_copy(j).wait()
        log_mean[...] += jnp.dot(stream[j % 2], jnp.ones((PART, 128), b16), preferred_element_type=f32)

        @pl.when(j + 2 < PARTS)
        def _():
            stream_copy(j + 2).start()
        return carry

    lax.fori_loop(0, PARTS, add_means, 0)
    log_mean[...] = jnp.log(log_mean[...] / pixel_count)
    gather(2)(0)
    load.wait()

    def take_logs(h):
        def body(j, carry):
            rows = pl.ds(pl.multiple_of(j * 16, 16), 16)
            logs[h, rows, :] = jnp.log(part[pl.ds(pl.multiple_of(h * HALF + j * 16, 16), 16), :].astype(f32)).astype(b16)
            return carry
        lax.fori_loop(0, HALF // 16, body, 0)
        logs[h, HALF:HELD, :] = jnp.ones((HELD - HALF, PART), b16)

    take_logs(0)
    gather(3)(0)
    gather(1)(1)
    take_logs(1)
    gather(2)(1)
    gather(1)(2)
    weight = interp_ref[...]
    weight_hi = weight.astype(b16)
    weight_lo = (weight - weight_hi.astype(f32)).astype(b16)

    def spread(j, carry):
        lane = lax.broadcasted_iota(jnp.int32, (128, 256), 0)
        column_of = plane * 16 + 2 * j + lax.broadcasted_iota(jnp.int32, (128, 256), 1) // 128
        hot = jnp.where(lane == column_of, 1.0, 0.0).astype(b16)
        out = jnp.dot(weight_hi, hot, preferred_element_type=f32) + jnp.dot(weight_lo, hot, preferred_element_type=f32)
        rows_ref[2 * j] = out[:, :128]
        rows_ref[2 * j + 1] = out[:, 128:]
        return carry

    lax.fori_loop(0, PARTS, spread, 0)
    mass[...] = jnp.zeros_like(mass)
    voxel_weight_ref[...] = jnp.zeros_like(voxel_weight_ref)
    index_rows[...] = index_ref[...].astype(f32).T
    weight_rows[...] = weight.T
    first_q = pl.ds(pl.multiple_of(plane * 16, 16), 16)
    index_part, weight_part = index_rows[first_q, :], weight_rows[first_q, :]
    for q in range(16):
        index_rows[8 * q:8 * q + 8] = jnp.broadcast_to(index_part[q:q + 1], (8, 2 * HALF))
        weight_rows[8 * q:8 * q + 8] = jnp.broadcast_to(weight_part[q:q + 1], (8, 2 * HALF))

    def clear(j, carry):
        some = pl.ds(pl.multiple_of(j * 16, 16), 16)
        gathered[some, :] = 0.25 * part[some, :].astype(f32)
        return carry

    lax.fori_loop(0, 2 * HALF // 16, clear, 0)

    def pair_copy(s):
        return remote(scores.at[s % 2, 1 - core], pair_in.at[s], pair_sem.at[0, s], pair_sem.at[1, s], sibling)

    def z1_copies(s):
        return (remote(blocks_a.at[s % 2, 1 - group], z1a_in.at[s], z1a_sem.at[0, s], z1a_sem.at[1, s], near),
                remote(blocks_b.at[s % 2, 1 - spot], z1b_in.at[s], z1b_sem.at[0, s], z1b_sem.at[1, s], far))

    def z2_copies(s):
        return (remote(kept_a.at[s % 2, 1 - spot], z2a_in.at[s], z2a_sem.at[0, s], z2a_sem.at[1, s], far),
                remote(kept_b.at[s % 2, 1 - z % 2], z2b_in.at[s], z2b_sem.at[0, s], z2b_sem.at[1, s], near))

    def sib_copy(s):
        return remote(stat.at[s % 2], sib_in.at[s], sib_sem.at[0, s], sib_sem.at[1, s], sibling)

    def x_copy(s, d):
        return remote(stat2.at[s % 2], x_in.at[s, d - 1], x_send.at[s, d - 1], x_recv.at[s, d - 1], moved(me, 0, d))

    def y_copy(s, d):
        return remote(stat3.at[s % 2], y_in.at[s, d - 1], y_send.at[s, d - 1], y_recv.at[s, d - 1], moved(me, 1, d))

    def ag_copies(s):
        lanes = pl.ds(pl.multiple_of(z * 128, 128), 128)
        return [remote(prob.at[s, core, :, lanes], prob.at[s, core, :, lanes], ag_send.at[s, d - 1], ag_recv.at[s, d - 1],
                       moved(me, 2, d)) for d in (1, 2, 3)]

    def agc_copy(s):
        return remote(prob.at[s, core], prob.at[s, core], agc_sem.at[0, s], agc_sem.at[1, s], sibling)

    def multiply(s):
        pl.when(s >= 2)(lambda: pair_copy(s - 2).wait_send())

        def tile(j, carry):
            block = frames[s, pl.ds(2 * j, 2)].reshape(HALF, PART)
            lanes = pl.ds(pl.multiple_of(j * HALF, HALF), HALF)
            for h in range(2):
                scores[s % 2, h, :, lanes] = lax.dot_general(logs[h], block, NT, preferred_element_type=f32)
            return carry

        lax.fori_loop(0, 2, tile, 0)
        pair_copy(s).start()

    def settle(copies):
        for copy in copies:
            copy.wait_send()

    def add_pair(s):
        pl.when(s >= 2)(lambda: settle(z1_copies(s - 2)))
        pair_copy(s).wait_recv()
        for b, (g, n) in enumerate(((0, 0), (1, 0), (1, 1), (0, 1))):
            lanes = slice(128 * b, 128 * b + 128)
            total = scores[s % 2, core, :, lanes] + pair_in[s, :, lanes]
            blocks_a[s % 2, g, n] = total[:CUT]
            blocks_b[s % 2, b // 2, b % 2] = total[CUT:]
        for copy in z1_copies(s):
            copy.start()

    def add_first(s):
        pl.when(s >= 2)(lambda: settle(z2_copies(s - 2)))
        for copy in z1_copies(s):
            copy.wait_recv()
        kept_a[s % 2] = blocks_a[s % 2, group] + z1a_in[s]
        kept_b[s % 2] = blocks_b[s % 2, spot] + z1b_in[s]
        for copy in z2_copies(s):
            copy.start()

    first_row = lax.broadcasted_iota(jnp.int32, (8, 128), 0) == 0

    def combine(tiles):
        peak = tiles[0][0:1]
        for tile in tiles[1:]:
            peak = jnp.maximum(peak, tile[0:1])
        total = sum(tile[1:2] * jnp.exp(tile[0:1] - peak) for tile in tiles)
        return peak, total

    def score(s):
        pl.when(s >= 2)(lambda: sib_copy(s - 2).wait_send())
        for copy in z2_copies(s):
            copy.wait_recv()
        upper = kept_a[s % 2, spot] + z2a_in[s]
        lower = kept_b[s % 2, z % 2] + z2b_in[s]
        photons = lower[HALF - CUT:HALF - CUT + 1]
        value = jnp.concatenate([upper, lower[:HALF - CUT]], axis=0)
        value = (value - photons * log_mean[...]) * (score_beta / pixel_count)
        peak = jnp.max(value, axis=0, keepdims=True)
        value = jnp.exp(value - peak)
        shifted[s % 2] = value
        photon[s % 2] = jnp.broadcast_to(photons, (8, 128))
        stat[s % 2] = jnp.where(first_row, peak, jnp.sum(value, axis=0, keepdims=True))
        sib_copy(s).start()

    def add_sibling(s):
        pl.when(s >= 2)(lambda: settle([x_copy(s - 2, d) for d in (1, 2, 3)]))
        sib_copy(s).wait_recv()
        peak, total = combine([stat[s % 2], sib_in[s]])
        stat2[s % 2] = jnp.where(first_row, peak, total)
        for d in (1, 2, 3):
            x_copy(s, d).start()

    def add_x(s):
        pl.when(s >= 2)(lambda: settle([y_copy(s - 2, d) for d in (1, 2, 3)]))
        for d in (1, 2, 3):
            x_copy(s, d).wait_recv()
        peak, total = combine([stat2[s % 2], x_in[s, 0], x_in[s, 1], x_in[s, 2]])
        stat3[s % 2] = jnp.where(first_row, peak, total)
        for d in (1, 2, 3):
            y_copy(s, d).start()

    def normalise(s):
        for d in (1, 2, 3):
            y_copy(s, d).wait_recv()
        peak, total = combine([stat3[s % 2], y_in[s, 0], y_in[s, 1], y_in[s, 2]])
        factor = jnp.exp(stat[s % 2][0:1] - peak) / total
        lanes = pl.ds(pl.multiple_of(z * 128, 128), 128)
        prob[s, core, :HALF, lanes] = (shifted[s % 2] * factor).astype(b16)
        photons = photon[s % 2][0:1]
        upper = photons.astype(b16).astype(f32)
        row = lax.broadcasted_iota(jnp.int32, (HELD - HALF, 128), 0)
        prob[s, core, HALF:, lanes] = jnp.where(row == 0, upper, jnp.where(row == 1, photons - upper, 0.0)).astype(b16)
        for copy in ag_copies(s):
            copy.start()

    def share_pair(s):
        for copy in ag_copies(s):
            copy.wait_recv()
        agc_copy(s).start()

    def gather_pixels(s):
        agc_copy(s).wait_recv()
        for h in range(2):
            mass[h] += lax.dot_general(prob[s, h, :HALF], prob[s, 0, HALF:], NT, preferred_element_type=f32)

        def tile(j, carry):
            lanes = pl.ds(pl.multiple_of(j * 256, 256), 256)
            block = frames[s, :, :, :, lanes].reshape(2 * HALF, 256)
            for h in range(2):
                gathered[h * HALF:h * HALF + HALF, lanes] += jnp.dot(prob[s, h, :HALF], block, preferred_element_type=f32)
            return carry

        lax.fori_loop(0, PARTS, tile, 0)

    def weigh(t):
        for q in (2 * t, 2 * t + 1):
            rows = pl.ds(pl.multiple_of(q * 8, 8), 8)
            target = index_rows[rows, :][0:1].astype(jnp.int32)
            amount = weight_rows[rows, :][0:1]
            owner = (target * 43691) >> 21
            lower = target - 48 * owner
            slot = (owner & 1) * 64 + (owner >> 1)
            row = lax.broadcasted_iota(jnp.int32, (128, 2 * HALF), 0)
            amount_hi = amount.astype(b16).astype(f32)
            hot = jnp.where(row == slot, 1.0, 0.0).astype(b16)
            parts = jnp.concatenate([jnp.where(row == lower, amount_hi, 0.0).astype(b16),
                                     jnp.where(row == lower, amount - amount_hi, 0.0).astype(b16)], axis=0)
            out = lax.dot_general(hot, parts, NT, preferred_element_type=f32)
            voxel_weight_ref[...] += out[:, :128] + out[:, 128:]

    def tick(t, carry):
        when(t + 1, gather(4))
        when(t - 2, add_pair)
        when(t - 3, score)
        when(t - 4, add_x)
        when(t + 2, gather(3))
        when(t + 3, gather(2))
        when(t + 4, gather(1))
        when(t - 5, share_pair)
        when(t, gather(5))
        when(t - 3, add_sibling)
        when(t - 1, multiply)
        when(t - 2, add_first)
        when(t, weigh)
        when(t - 4, normalise)
        when(t - 5, gather_pixels)
        return carry

    lax.fori_loop(-1, PARTS + 5, tick, 0)

    share = 1.0 / (jnp.sum(mass[...], axis=2, keepdims=True) * (1.0 / pixel_count) + 0.25)
    writes = []
    for q in range(PART // 128):
        for h in range(2):
            lanes, some = slice(128 * q, 128 * q + 128), slice(h * HALF, h * HALF + HALF)
            rows_ref[q, some] = rows_ref[q, some] * (gathered[some, lanes] * share[h])
        writes.append(pltpu.make_async_copy(rows_ref.at[q], rows_hbm.at[q], rows_sem.at[q]))
        writes[-1].start()

    def drain(i, carry):
        for n in range(16):
            gather_copy(i, n).wait_send()
        settle(ag_copies(i))
        agc_copy(i).wait_send()
        return carry

    lax.fori_loop(0, PARTS, drain, 0)

    def drain_a2a(d, carry):
        a2a_copy(d).wait_send()
        return carry

    lax.fori_loop(1, PARTS, drain_a2a, 0)
    for s in (PARTS - 2, PARTS - 1):
        pair_copy(s).wait_send()
        settle(z1_copies(s))
        settle(z2_copies(s))
        sib_copy(s).wait_send()
        for d in (1, 2, 3):
            x_copy(s, d).wait_send()
            y_copy(s, d).wait_send()
    for write in writes:
        write.wait()


def iterate(counts, gain, interp, index, slices):
    f32, b16 = jnp.float32, jnp.bfloat16
    vm, dma = pltpu.VMEM, pltpu.SemaphoreType.DMA
    n = PARTS
    scratch = [
        vm((32, n * PART), jnp.int32), vm((PART // 128, 2 * HALF, 128), f32), vm((128, 2 * HALF), f32), vm((128, 2 * HALF), f32),
        vm((n, 32, PART), b16), vm((n, 4, 4, 32, PART), b16), vm((2 * HALF, PART), b16), vm((2, HALF, PART), b16),
        vm((2, HELD, PART), b16), vm((HALF, 128), f32), vm((2, 2, HELD, 512), f32), vm((n, HELD, 512), f32),
        vm((2, 2, 2, CUT, 128), f32), vm((2, 2, 2, CUT, 128), f32), vm((n, 2, CUT, 128), f32), vm((n, 2, CUT, 128), f32),
        vm((2, 2, CUT, 128), f32), vm((2, 2, CUT, 128), f32), vm((n, CUT, 128), f32), vm((n, CUT, 128), f32),
        vm((2, HALF, 128), f32), vm((2, 8, 128), f32), vm((2, 8, 128), f32), vm((2, 8, 128), f32), vm((2, 8, 128), f32),
        vm((n, 8, 128), f32), vm((n, 3, 8, 128), f32), vm((n, 3, 8, 128), f32),
        vm((n, 2, HELD, 512), b16), vm((2 * HALF, PART), f32), vm((2, HALF, HELD - HALF), f32),
        dma((4,)), dma((PART // 128,)), dma((n - 1,)), dma((n,)), dma((n, 16)), dma((n, 16)),
        dma((2, n)), dma((2, n)), dma((2, n)), dma((2, n)), dma((2, n)), dma((2, n)),
        dma((n, 3)), dma((n, 3)), dma((n, 3)), dma((n, 3)), dma((n, 3)), dma((n, 3)), dma((2, n)),
    ]
    vspec, anyspec = pl.BlockSpec(memory_space=pltpu.VMEM), pl.BlockSpec(memory_space=pl.ANY)
    return pl.pallas_call(
        iterate_kernel,
        out_shape=[jax.ShapeDtypeStruct((PART // 128, 2 * HALF, 128), f32), jax.ShapeDtypeStruct((128, 128), f32)],
        in_specs=[anyspec, vspec, vspec, vspec, anyspec], out_specs=[anyspec, vspec], scratch_shapes=scratch,
        compiler_params=pltpu.CompilerParams(collective_id=2, has_side_effects=True, vmem_limit_bytes=62 * 2**20),
    )(counts, gain.reshape(1, -1), interp, index, slices)


def scatter_kernel(q_count, rows_ref, index_hbm, out_ref, index_smem, sem, *accs):
    copy = pltpu.make_async_copy(index_hbm, index_smem, sem)
    copy.start()
    voxels = out_ref.shape[0]
    orients = rows_ref.shape[1]

    def clear(t, carry):
        for acc in accs:
            acc[pl.ds(pl.multiple_of(t * 64, 64), 64), :] = jnp.zeros((64, 128), jnp.float32)
        return carry

    lax.fori_loop(0, voxels // 64, clear, 0)
    copy.wait()
    base = lax.axis_index("frame") * q_count

    def step(t, carry):
        n = 0
        for q in range(q_count):
            for s in range(8):
                r = t * 8 + s
                i = index_smem[r, base + q]
                acc = accs[n % len(accs)]
                n += 1
                acc[pl.ds(i, 1), :] += rows_ref[q, pl.ds(r, 1), :]
        return carry

    lax.fori_loop(0, orients // 8, step, 0)

    def finish(t, carry):
        d = pl.ds(pl.multiple_of(t * 64, 64), 64)
        total = accs[0][d, :]
        for acc in accs[1:]:
            total = total + acc[d, :]
        out_ref[d, :] = total
        return carry

    lax.fori_loop(0, voxels // 64, finish, 0)


def scatter(rows, index, voxels):
    q_count = rows.shape[0]
    return pl.pallas_call(
        functools.partial(scatter_kernel, q_count),
        out_shape=jax.ShapeDtypeStruct((voxels, 128), jnp.float32),
        in_specs=[
            pl.BlockSpec(memory_space=pltpu.VMEM),
            pl.BlockSpec(memory_space=pl.ANY),
        ],
        out_specs=pl.BlockSpec(memory_space=pltpu.VMEM),
        scratch_shapes=[pltpu.SMEM(index.shape, jnp.int32), pltpu.SemaphoreType.DMA]
        + [pltpu.VMEM((voxels, 128), jnp.float32)] * ACCS,
        compiler_params=pltpu.CompilerParams(vmem_limit_bytes=48 * 2**20),
    )(rows, index)


def local(counts, pixel_gain, slices, voxel_index, interp):
    voxels = VB_DEV * lax.axis_size("orient") * lax.axis_size("frame")
    rows, voxel_weight = iterate(counts, pixel_gain, interp, voxel_index, slices)
    voxel_sum = scatter(rows, voxel_index, voxels)
    return reduce_blocks(
        voxel_sum.reshape(SIDE, SIDE, SIDE, 2, VB_DEV, 128), voxel_weight.reshape(2, SIDE, SIDE * SIDE, 128)
    )


def solution(mesh):
    placed = (
        P(("orient", "frame"), None),
        P(),
        P("orient", None),
        P("orient", None),
        P("orient", None),
    )
    return jax.shard_map(
        local, mesh=mesh, in_specs=placed, out_specs=P(("orient", "frame"), None), check_vma=False
    )
```

```python
import functools

import jax
import jax.numpy as jnp
from jax import lax
from jax.experimental import pallas as pl
from jax.experimental.pallas import tpu as pltpu
from jax.sharding import PartitionSpec as P

VB_DEV = 48
ACCS = 4


SIDE = 4
ORDERS = ((0, 1, 2), (1, 2, 0), (2, 0, 1))


def here():
    orient, frame = lax.axis_index("orient"), lax.axis_index("frame")
    return (orient // SIDE, orient % SIDE, frame // 2, frame % 2)


def device(place):
    x, y, z, core = place
    return (x * SIDE + y, z * 2 + core)


def moved(place, axis, step):
    out = list(place)
    out[axis] = (place[axis] + step) % SIDE
    return tuple(out)


def pick(ref, axis, value, ndim):
    return ref.at[tuple(value if a == axis else slice(None) for a in range(ndim))]


def sums_kernel(v_ref, w_ref, o_ref, pair_out, pair_in, s1, s1b, in1, s2, s2b, in2, s3, s3b, in3,
                wsum, wpair_in, win1, w2, win2, w3, win3,
                pair_sem, sem1, sem2, sem3, wpair_sem, wsem1, wsem2, wsem3):
    me = here()
    core = me[3]
    sibling = (me[0], me[1], me[2], 1 - core)
    barrier = pltpu.get_barrier_semaphore()
    peers = [sibling] + [moved(me, a, d) for a in range(3) for d in (1, 2, 3)]
    for peer in peers:
        pl.semaphore_signal(barrier, inc=1, device_id=device(peer), device_id_type=pl.DeviceIdType.MESH)
    for p in range(3):
        pair_out[p] = v_ref[:, :, :, 1 - core, 16 * p:16 * p + 16, :].astype(jnp.bfloat16)
    pl.semaphore_wait(barrier, len(peers))

    def send(src, dst, sems, slot, place):
        copy = pltpu.make_async_remote_copy(
            src_ref=src, dst_ref=dst, send_sem=sems.at[0, slot], recv_sem=sems.at[1, slot],
            device_id=device(place), device_id_type=pl.DeviceIdType.MESH)
        copy.start()
        return copy

    pair = [send(pair_out.at[p], pair_in.at[p], pair_sem, p, sibling) for p in range(3)]
    wpair = send(w_ref.at[1 - core], wpair_in, wpair_sem, 0, sibling)
    first, second, third = [], [], []
    for p in range(3):
        axis = ORDERS[p][0]
        pair[p].wait_recv()
        total = v_ref[:, :, :, core, 16 * p:16 * p + 16, :] + pair_in[p].astype(jnp.float32)
        s1[p] = total
        s1b[p] = total.astype(jnp.bfloat16)
        first.append([send(pick(s1b.at[p], axis, (me[axis] + d) % SIDE, 3), in1.at[p, d - 1], sem1, 3 * p + d - 1,
                           moved(me, axis, d)) for d in (1, 2, 3)])
    wpair.wait_recv()
    wsum[...] = w_ref[core] + wpair_in[...]
    wfirst = [send(wsum.at[(me[0] + d) % SIDE], win1.at[d - 1], wsem1, d - 1, moved(me, 0, d)) for d in (1, 2, 3)]
    for p in range(3):
        axis, nxt = ORDERS[p][0], ORDERS[p][1]
        for copy in first[p]:
            copy.wait_recv()
        own = pick(s1.at[p], axis, me[axis], 3)[...]
        total = own + in1[p, 0].astype(jnp.float32) + in1[p, 1].astype(jnp.float32) + in1[p, 2].astype(jnp.float32)
        s2[p] = total
        s2b[p] = total.astype(jnp.bfloat16)
        dim = nxt - (1 if nxt > axis else 0)
        second.append([send(pick(s2b.at[p], dim, (me[nxt] + d) % SIDE, 2), in2.at[p, d - 1], sem2, 3 * p + d - 1,
                            moved(me, nxt, d)) for d in (1, 2, 3)])
    for copy in wfirst:
        copy.wait_recv()
    w2[...] = wsum[me[0]] + win1[0] + win1[1] + win1[2]
    wsecond = [send(w2, win2.at[d - 1], wsem2, d - 1, moved(me, 1, d)) for d in (1, 2, 3)]
    for p in range(3):
        axis, nxt, last = ORDERS[p]
        for copy in second[p]:
            copy.wait_recv()
        dim = nxt - (1 if nxt > axis else 0)
        own = pick(s2.at[p], dim, me[nxt], 2)[...]
        total = own + in2[p, 0].astype(jnp.float32) + in2[p, 1].astype(jnp.float32) + in2[p, 2].astype(jnp.float32)
        s3[p] = total
        s3b[p] = total.astype(jnp.bfloat16)
        third.append([send(s3b.at[p, (me[last] + d) % SIDE], in3.at[p, d - 1], sem3, 3 * p + d - 1,
                           moved(me, last, d)) for d in (1, 2, 3)])
    for copy in wsecond:
        copy.wait_recv()
    w3[...] = w2[...] + win2[0] + win2[1] + win2[2]
    wthird = [send(w3, win3.at[d - 1], wsem3, d - 1, moved(me, 2, d)) for d in (1, 2, 3)]
    for copy in wthird:
        copy.wait_recv()
    weights = w3[...] + win3[0] + win3[1] + win3[2]
    mine = lax.broadcasted_iota(jnp.int32, weights.shape, 0) == me[1] * SIDE + me[2]
    row = jnp.sum(jnp.where(mine, weights, 0.0), axis=0, keepdims=True)
    shape = (o_ref.shape[0], 128)
    diagonal = lax.broadcasted_iota(jnp.int32, shape, 0) == lax.broadcasted_iota(jnp.int32, shape, 1)
    column = jnp.sum(jnp.where(diagonal, row, 0.0), axis=1, keepdims=True)
    scale = 1.0 / (1.0 + column)
    for p in range(3):
        for copy in third[p]:
            copy.wait_recv()
        own = s3[p, me[ORDERS[p][2]]]
        total = own + in3[p, 0].astype(jnp.float32) + in3[p, 1].astype(jnp.float32) + in3[p, 2].astype(jnp.float32)
        o_ref[16 * p:16 * p + 16, :] = total * scale[16 * p:16 * p + 16]
    for copies in pair, [wpair], *first, *second, *third, wfirst, wsecond, wthird:
        for copy in copies:
            copy.wait_send()


def reduce_blocks(voxel_sum, voxel_weight):
    f32, b16 = jnp.float32, jnp.bfloat16
    vm, dma = pltpu.VMEM, pltpu.SemaphoreType.DMA
    scratch = [
        vm((3, 4, 4, 4, 16, 128), b16), vm((3, 4, 4, 4, 16, 128), b16),
        vm((3, 4, 4, 4, 16, 128), f32), vm((3, 4, 4, 4, 16, 128), b16), vm((3, 3, 4, 4, 16, 128), b16),
        vm((3, 4, 4, 16, 128), f32), vm((3, 4, 4, 16, 128), b16), vm((3, 3, 4, 16, 128), b16),
        vm((3, 4, 16, 128), f32), vm((3, 4, 16, 128), b16), vm((3, 3, 16, 128), b16),
        vm((4, 16, 128), f32), vm((4, 16, 128), f32), vm((3, 16, 128), f32),
        vm((16, 128), f32), vm((3, 16, 128), f32), vm((16, 128), f32), vm((3, 16, 128), f32),
        dma((2, 3)), dma((2, 9)), dma((2, 9)), dma((2, 9)), dma((2, 1)), dma((2, 3)), dma((2, 3)), dma((2, 3)),
    ]
    vspec = pl.BlockSpec(memory_space=pltpu.VMEM)
    return pl.pallas_call(
        sums_kernel,
        out_shape=jax.ShapeDtypeStruct((48, 128), f32),
        in_specs=[vspec, vspec], out_specs=vspec, scratch_shapes=scratch,
        compiler_params=pltpu.CompilerParams(collective_id=3, has_side_effects=True, vmem_limit_bytes=40 * 2**20),
    )(voxel_sum, voxel_weight)


PARTS = 8
PART = 2048
HALF = 256
HELD = 272
CUT = 136
score_beta = 1.5
NT = (((1,), (1,)), ((), ()))


def iterate_kernel(counts_hbm, gain_ref, interp_ref, index_ref, slices_hbm, rows_hbm, voxel_weight_ref,
                   counts_ref, rows_ref, index_rows, weight_rows,
                   own, frames, part, stream, logs, log_mean, scores, pair_in, blocks_a, blocks_b, z1a_in, z1b_in, kept_a, kept_b, z2a_in, z2b_in,
                   shifted, photon, stat, stat2, stat3, sib_in, x_in, y_in, prob, gathered, mass,
                   load_sem, rows_sem, a2a_send, a2a_recv, g_send, g_recv, pair_sem, z1a_sem, z1b_sem, z2a_sem, z2b_sem, sib_sem,
                   x_send, x_recv, y_send, y_recv, ag_send, ag_recv, agc_sem):
    f32, b16 = jnp.float32, jnp.bfloat16
    x, y, z, core = me = here()
    plane = z * 2 + core
    pixel_count = PARTS * PART
    sibling = (x, y, z, 1 - core)
    near = (x, y, z + 1 - 2 * (z % 2), core)
    far = (x, y, 3 - z, core)
    group = ((z + 1) // 2) % 2
    spot = z // 2
    xl, xr, yl, yr = (x + 3) % 4, (x + 1) % 4, (y + 3) % 4, (y + 1) % 4
    to_xr, to_xl = (xr, y, z, core), (xl, y, z, core)
    to_yr, to_yl = (x, yr, z, core), (x, yl, z, core)

    def remote(src, dst, send_sem, recv_sem, place):
        return pltpu.make_async_remote_copy(
            src_ref=src, dst_ref=dst, send_sem=send_sem, recv_sem=recv_sem,
            device_id=device(place), device_id_type=pl.DeviceIdType.MESH)

    def when(s, body, limit=PARTS):
        pl.when((s >= 0) & (s < limit))(lambda: body(s))

    count_copy = pltpu.make_async_copy(counts_hbm, counts_ref, load_sem.at[3])
    count_copy.start()
    load = pltpu.make_async_copy(
        slices_hbm.at[:, pl.ds(pl.multiple_of(plane * PART, PART), PART)], part, load_sem.at[0])
    load.start()

    def stream_copy(j):
        return pltpu.make_async_copy(
            slices_hbm.at[pl.ds(pl.multiple_of(core * HALF, HALF), HALF), pl.ds(pl.multiple_of(j * PART, PART), PART)],
            stream.at[j % 2], load_sem.at[1 + j % 2])

    stream_copy(0).start()
    stream_copy(1).start()

    barrier = pltpu.get_barrier_semaphore()
    column = [(plane + d) % PARTS for d in range(1, PARTS)]
    peers = [(x, y, k // 2, k % 2) for k in column]
    peers += [moved(me, 0, d) for d in (1, 2, 3)] + [moved(me, 1, d) for d in (1, 2, 3)]
    for peer in peers:
        pl.semaphore_signal(barrier, inc=1, device_id=device(peer), device_id_type=pl.DeviceIdType.MESH)

    def correct(j, carry):
        lanes = pl.ds(pl.multiple_of(j * PART, PART), PART)
        own[j] = (counts_ref[:, lanes].astype(f32) * gain_ref[:, lanes]).astype(b16)
        return carry

    count_copy.wait()
    lax.fori_loop(0, PARTS, correct, 0)
    frames[plane, x, y] = own[plane]
    pl.semaphore_wait(barrier, len(peers))

    def a2a_copy(d):
        k = (plane + d) % PARTS
        return remote(own.at[k], frames.at[plane, x, y], a2a_send.at[d - 1], a2a_recv.at[plane], (x, y, k // 2, k % 2))

    def a2a_start(d, carry):
        a2a_copy(d).start()
        return carry

    lax.fori_loop(1, PARTS, a2a_start, 0)

    def order(i):
        return jnp.where(i == 0, plane, jnp.where(i - 1 < plane, i - 1, i))

    def gather_copy(i, n):
        s = order(i)
        lo, hi = pl.ds(0, 16), pl.ds(16, 16)
        left, right = pl.ds(0, PART // 2), pl.ds(PART // 2, PART // 2)
        two, other = pl.ds(0, 2), pl.ds(2, 2)
        every = pl.ds(0, 4)
        full = pl.ds(0, PART)
        where, place = [
            ((s, x, y, lo, full), to_xr), ((s, x, y, lo, full), to_xl),
            ((s, x, y, hi, full), to_yr), ((s, x, y, hi, full), to_yl),
            ((s, xl, y, lo, left), to_xr), ((s, xr, y, lo, right), to_xl),
            ((s, x, yl, hi, left), to_yr), ((s, x, yr, hi, right), to_yl),
            ((s, every, y, lo, full), to_yr), ((s, every, y, lo, full), to_yl),
            ((s, x, every, hi, full), to_xr), ((s, x, every, hi, full), to_xl),
            ((s, two, yl, lo, full), to_yr), ((s, other, yr, lo, full), to_yl),
            ((s, xl, two, hi, full), to_xr), ((s, xr, other, hi, full), to_xl),
        ][n]
        return remote(frames.at[where], frames.at[where], g_send.at[i, n], g_recv.at[i, n], place)

    def gather(stage):
        def body(i):
            if stage == 1:
                s = order(i)

                @pl.when(s != plane)
                def _():
                    remote(own.at[0], frames.at[s, x, y], a2a_send.at[0], a2a_recv.at[s], sibling).wait_recv()
            else:
                for n in range(4 * stage - 8, 4 * stage - 4):
                    gather_copy(i, n).wait_recv()
            if stage < 5:
                for n in range(4 * stage - 4, 4 * stage):
                    gather_copy(i, n).start()
        return body

    when(0, gather(1))

    log_mean[...] = jnp.zeros_like(log_mean)

    def add_means(j, carry):
        stream_copy(j).wait()
        log_mean[...] += jnp.dot(stream[j % 2], jnp.ones((PART, 128), b16), preferred_element_type=f32)

        @pl.when(j + 2 < PARTS)
        def _():
            stream_copy(j + 2).start()
        return carry

    lax.fori_loop(0, PARTS, add_means, 0)
    log_mean[...] = jnp.log(log_mean[...] / pixel_count)
    gather(2)(0)
    load.wait()

    def take_logs(h):
        def body(j, carry):
            rows = pl.ds(pl.multiple_of(j * 16, 16), 16)
            logs[h, rows, :] = jnp.log(part[pl.ds(pl.multiple_of(h * HALF + j * 16, 16), 16), :].astype(f32)).astype(b16)
            return carry
        lax.fori_loop(0, HALF // 16, body, 0)
        logs[h, HALF:HELD, :] = jnp.ones((HELD - HALF, PART), b16)

    take_logs(0)
    gather(3)(0)
    gather(1)(1)
    take_logs(1)
    gather(2)(1)
    gather(1)(2)
    weight = interp_ref[...]
    weight_hi = weight.astype(b16)
    weight_lo = (weight - weight_hi.astype(f32)).astype(b16)

    def spread(j, carry):
        lane = lax.broadcasted_iota(jnp.int32, (128, 256), 0)
        column_of = plane * 16 + 2 * j + lax.broadcasted_iota(jnp.int32, (128, 256), 1) // 128
        hot = jnp.where(lane == column_of, 1.0, 0.0).astype(b16)
        out = jnp.dot(weight_hi, hot, preferred_element_type=f32) + jnp.dot(weight_lo, hot, preferred_element_type=f32)
        rows_ref[2 * j] = out[:, :128]
        rows_ref[2 * j + 1] = out[:, 128:]
        return carry

    lax.fori_loop(0, PARTS, spread, 0)
    mass[...] = jnp.zeros_like(mass)
    voxel_weight_ref[...] = jnp.zeros_like(voxel_weight_ref)
    index_rows[...] = index_ref[...].astype(f32).T
    weight_rows[...] = weight.T
    first_q = pl.ds(pl.multiple_of(plane * 16, 16), 16)
    index_part, weight_part = index_rows[first_q, :], weight_rows[first_q, :]
    for q in range(16):
        index_rows[8 * q:8 * q + 8] = jnp.broadcast_to(index_part[q:q + 1], (8, 2 * HALF))
        weight_rows[8 * q:8 * q + 8] = jnp.broadcast_to(weight_part[q:q + 1], (8, 2 * HALF))

    def clear(j, carry):
        some = pl.ds(pl.multiple_of(j * 16, 16), 16)
        gathered[some, :] = 0.25 * part[some, :].astype(f32)
        return carry

    lax.fori_loop(0, 2 * HALF // 16, clear, 0)

    def pair_copy(s):
        return remote(scores.at[s % 2, 1 - core], pair_in.at[s], pair_sem.at[0, s], pair_sem.at[1, s], sibling)

    def z1_copies(s):
        return (remote(blocks_a.at[s % 2, 1 - group], z1a_in.at[s], z1a_sem.at[0, s], z1a_sem.at[1, s], near),
                remote(blocks_b.at[s % 2, 1 - spot], z1b_in.at[s], z1b_sem.at[0, s], z1b_sem.at[1, s], far))

    def z2_copies(s):
        return (remote(kept_a.at[s % 2, 1 - spot], z2a_in.at[s], z2a_sem.at[0, s], z2a_sem.at[1, s], far),
                remote(kept_b.at[s % 2, 1 - z % 2], z2b_in.at[s], z2b_sem.at[0, s], z2b_sem.at[1, s], near))

    def sib_copy(s):
        return remote(stat.at[s % 2], sib_in.at[s], sib_sem.at[0, s], sib_sem.at[1, s], sibling)

    def x_copy(s, d):
        return remote(stat2.at[s % 2], x_in.at[s, d - 1], x_send.at[s, d - 1], x_recv.at[s, d - 1], moved(me, 0, d))

    def y_copy(s, d):
        return remote(stat3.at[s % 2], y_in.at[s, d - 1], y_send.at[s, d - 1], y_recv.at[s, d - 1], moved(me, 1, d))

    def ag_copies(s):
        lanes = pl.ds(pl.multiple_of(z * 128, 128), 128)
        return [remote(prob.at[s, core, :, lanes], prob.at[s, core, :, lanes], ag_send.at[s, d - 1], ag_recv.at[s, d - 1],
                       moved(me, 2, d)) for d in (1, 2, 3)]

    def agc_copy(s):
        return remote(prob.at[s, core], prob.at[s, core], agc_sem.at[0, s], agc_sem.at[1, s], sibling)

    def multiply(s):
        pl.when(s >= 2)(lambda: pair_copy(s - 2).wait_send())

        def tile(j, carry):
            block = frames[s, pl.ds(2 * j, 2)].reshape(HALF, PART)
            lanes = pl.ds(pl.multiple_of(j * HALF, HALF), HALF)
            for h in range(2):
                scores[s % 2, h, :, lanes] = lax.dot_general(logs[h], block, NT, preferred_element_type=f32)
            return carry

        lax.fori_loop(0, 2, tile, 0)
        pair_copy(s).start()

    def settle(copies):
        for copy in copies:
            copy.wait_send()

    def add_pair(s):
        pl.when(s >= 2)(lambda: settle(z1_copies(s - 2)))
        pair_copy(s).wait_recv()
        for b, (g, n) in enumerate(((0, 0), (1, 0), (1, 1), (0, 1))):
            lanes = slice(128 * b, 128 * b + 128)
            total = scores[s % 2, core, :, lanes] + pair_in[s, :, lanes]
            blocks_a[s % 2, g, n] = total[:CUT]
            blocks_b[s % 2, b // 2, b % 2] = total[CUT:]
        for copy in z1_copies(s):
            copy.start()

    def add_first(s):
        pl.when(s >= 2)(lambda: settle(z2_copies(s - 2)))
        for copy in z1_copies(s):
            copy.wait_recv()
        kept_a[s % 2] = blocks_a[s % 2, group] + z1a_in[s]
        kept_b[s % 2] = blocks_b[s % 2, spot] + z1b_in[s]
        for copy in z2_copies(s):
            copy.start()

    first_row = lax.broadcasted_iota(jnp.int32, (8, 128), 0) == 0

    def combine(tiles):
        peak = tiles[0][0:1]
        for tile in tiles[1:]:
            peak = jnp.maximum(peak, tile[0:1])
        total = sum(tile[1:2] * jnp.exp(tile[0:1] - peak) for tile in tiles)
        return peak, total

    def score(s):
        pl.when(s >= 2)(lambda: sib_copy(s - 2).wait_send())
        for copy in z2_copies(s):
            copy.wait_recv()
        upper = kept_a[s % 2, spot] + z2a_in[s]
        lower = kept_b[s % 2, z % 2] + z2b_in[s]
        photons = lower[HALF - CUT:HALF - CUT + 1]
        value = jnp.concatenate([upper, lower[:HALF - CUT]], axis=0)
        value = (value - photons * log_mean[...]) * (score_beta / pixel_count)
        peak = jnp.max(value, axis=0, keepdims=True)
        value = jnp.exp(value - peak)
        shifted[s % 2] = value
        photon[s % 2] = jnp.broadcast_to(photons, (8, 128))
        stat[s % 2] = jnp.where(first_row, peak, jnp.sum(value, axis=0, keepdims=True))
        sib_copy(s).start()

    def add_sibling(s):
        pl.when(s >= 2)(lambda: settle([x_copy(s - 2, d) for d in (1, 2, 3)]))
        sib_copy(s).wait_recv()
        peak, total = combine([stat[s % 2], sib_in[s]])
        stat2[s % 2] = jnp.where(first_row, peak, total)
        for d in (1, 2, 3):
            x_copy(s, d).start()

    def add_x(s):
        pl.when(s >= 2)(lambda: settle([y_copy(s - 2, d) for d in (1, 2, 3)]))
        for d in (1, 2, 3):
            x_copy(s, d).wait_recv()
        peak, total = combine([stat2[s % 2], x_in[s, 0], x_in[s, 1], x_in[s, 2]])
        stat3[s % 2] = jnp.where(first_row, peak, total)
        for d in (1, 2, 3):
            y_copy(s, d).start()

    def normalise(s):
        for d in (1, 2, 3):
            y_copy(s, d).wait_recv()
        peak, total = combine([stat3[s % 2], y_in[s, 0], y_in[s, 1], y_in[s, 2]])
        factor = jnp.exp(stat[s % 2][0:1] - peak) / total
        lanes = pl.ds(pl.multiple_of(z * 128, 128), 128)
        prob[s, core, :HALF, lanes] = (shifted[s % 2] * factor).astype(b16)
        photons = photon[s % 2][0:1]
        upper = photons.astype(b16).astype(f32)
        row = lax.broadcasted_iota(jnp.int32, (HELD - HALF, 128), 0)
        prob[s, core, HALF:, lanes] = jnp.where(row == 0, upper, jnp.where(row == 1, photons - upper, 0.0)).astype(b16)
        for copy in ag_copies(s):
            copy.start()

    def share_pair(s):
        for copy in ag_copies(s):
            copy.wait_recv()
        agc_copy(s).start()

    def gather_pixels(s):
        agc_copy(s).wait_recv()
        for h in range(2):
            mass[h] += lax.dot_general(prob[s, h, :HALF], prob[s, 0, HALF:], NT, preferred_element_type=f32)

        def tile(j, carry):
            lanes = pl.ds(pl.multiple_of(j * 256, 256), 256)
            block = frames[s, :, :, :, lanes].reshape(2 * HALF, 256)
            for h in range(2):
                gathered[h * HALF:h * HALF + HALF, lanes] += jnp.dot(prob[s, h, :HALF], block, preferred_element_type=f32)
            return carry

        lax.fori_loop(0, PARTS, tile, 0)

    def weigh(t):
        for q in (2 * t, 2 * t + 1):
            rows = pl.ds(pl.multiple_of(q * 8, 8), 8)
            target = index_rows[rows, :][0:1].astype(jnp.int32)
            amount = weight_rows[rows, :][0:1]
            owner = (target * 43691) >> 21
            lower = target - 48 * owner
            slot = (owner & 1) * 64 + (owner >> 1)
            row = lax.broadcasted_iota(jnp.int32, (128, 2 * HALF), 0)
            amount_hi = amount.astype(b16).astype(f32)
            hot = jnp.where(row == slot, 1.0, 0.0).astype(b16)
            parts = jnp.concatenate([jnp.where(row == lower, amount_hi, 0.0).astype(b16),
                                     jnp.where(row == lower, amount - amount_hi, 0.0).astype(b16)], axis=0)
            out = lax.dot_general(hot, parts, NT, preferred_element_type=f32)
            voxel_weight_ref[...] += out[:, :128] + out[:, 128:]

    def tick(t, carry):
        when(t + 1, gather(4))
        when(t - 2, add_pair)
        when(t - 3, score)
        when(t - 4, add_x)
        when(t + 2, gather(3))
        when(t + 3, gather(2))
        when(t + 4, gather(1))
        when(t - 5, share_pair)
        when(t, weigh)
        when(t, gather(5))
        when(t - 3, add_sibling)
        when(t - 1, multiply)
        when(t - 2, add_first)
        when(t - 4, normalise)
        when(t - 5, gather_pixels)
        return carry

    lax.fori_loop(-1, PARTS + 5, tick, 0)

    share = 1.0 / (jnp.sum(mass[...], axis=2, keepdims=True) * (1.0 / pixel_count) + 0.25)
    writes = []
    for q in range(PART // 128):
        for h in range(2):
            lanes, some = slice(128 * q, 128 * q + 128), slice(h * HALF, h * HALF + HALF)
            rows_ref[q, some] = rows_ref[q, some] * (gathered[some, lanes] * share[h])
        writes.append(pltpu.make_async_copy(rows_ref.at[q], rows_hbm.at[q], rows_sem.at[q]))
        writes[-1].start()

    def drain(i, carry):
        for n in range(16):
            gather_copy(i, n).wait_send()
        settle(ag_copies(i))
        agc_copy(i).wait_send()
        return carry

    lax.fori_loop(0, PARTS, drain, 0)

    def drain_a2a(d, carry):
        a2a_copy(d).wait_send()
        return carry

    lax.fori_loop(1, PARTS, drain_a2a, 0)
    for s in (PARTS - 2, PARTS - 1):
        pair_copy(s).wait_send()
        settle(z1_copies(s))
        settle(z2_copies(s))
        sib_copy(s).wait_send()
        for d in (1, 2, 3):
            x_copy(s, d).wait_send()
            y_copy(s, d).wait_send()
    for write in writes:
        write.wait()


def iterate(counts, gain, interp, index, slices):
    f32, b16 = jnp.float32, jnp.bfloat16
    vm, dma = pltpu.VMEM, pltpu.SemaphoreType.DMA
    n = PARTS
    scratch = [
        vm((32, n * PART), jnp.int32), vm((PART // 128, 2 * HALF, 128), f32), vm((128, 2 * HALF), f32), vm((128, 2 * HALF), f32),
        vm((n, 32, PART), b16), vm((n, 4, 4, 32, PART), b16), vm((2 * HALF, PART), b16), vm((2, HALF, PART), b16),
        vm((2, HELD, PART), b16), vm((HALF, 128), f32), vm((2, 2, HELD, 512), f32), vm((n, HELD, 512), f32),
        vm((2, 2, 2, CUT, 128), f32), vm((2, 2, 2, CUT, 128), f32), vm((n, 2, CUT, 128), f32), vm((n, 2, CUT, 128), f32),
        vm((2, 2, CUT, 128), f32), vm((2, 2, CUT, 128), f32), vm((n, CUT, 128), f32), vm((n, CUT, 128), f32),
        vm((2, HALF, 128), f32), vm((2, 8, 128), f32), vm((2, 8, 128), f32), vm((2, 8, 128), f32), vm((2, 8, 128), f32),
        vm((n, 8, 128), f32), vm((n, 3, 8, 128), f32), vm((n, 3, 8, 128), f32),
        vm((n, 2, HELD, 512), b16), vm((2 * HALF, PART), f32), vm((2, HALF, HELD - HALF), f32),
        dma((4,)), dma((PART // 128,)), dma((n - 1,)), dma((n,)), dma((n, 16)), dma((n, 16)),
        dma((2, n)), dma((2, n)), dma((2, n)), dma((2, n)), dma((2, n)), dma((2, n)),
        dma((n, 3)), dma((n, 3)), dma((n, 3)), dma((n, 3)), dma((n, 3)), dma((n, 3)), dma((2, n)),
    ]
    vspec, anyspec = pl.BlockSpec(memory_space=pltpu.VMEM), pl.BlockSpec(memory_space=pl.ANY)
    return pl.pallas_call(
        iterate_kernel,
        out_shape=[jax.ShapeDtypeStruct((PART // 128, 2 * HALF, 128), f32), jax.ShapeDtypeStruct((128, 128), f32)],
        in_specs=[anyspec, vspec, vspec, vspec, anyspec], out_specs=[anyspec, vspec], scratch_shapes=scratch,
        compiler_params=pltpu.CompilerParams(collective_id=2, has_side_effects=True, vmem_limit_bytes=62 * 2**20),
    )(counts, gain.reshape(1, -1), interp, index, slices)


def scatter_kernel(q_count, rows_ref, index_hbm, out_ref, index_smem, sem, *accs):
    copy = pltpu.make_async_copy(index_hbm, index_smem, sem)
    copy.start()
    voxels = out_ref.shape[0]
    orients = rows_ref.shape[1]

    def clear(t, carry):
        for acc in accs:
            acc[pl.ds(pl.multiple_of(t * 64, 64), 64), :] = jnp.zeros((64, 128), jnp.float32)
        return carry

    lax.fori_loop(0, voxels // 64, clear, 0)
    copy.wait()
    base = lax.axis_index("frame") * q_count

    def step(t, carry):
        n = 0
        for q in range(q_count):
            for s in range(8):
                r = t * 8 + s
                i = index_smem[r, base + q]
                acc = accs[n % len(accs)]
                n += 1
                acc[pl.ds(i, 1), :] += rows_ref[q, pl.ds(r, 1), :]
        return carry

    lax.fori_loop(0, orients // 8, step, 0)

    def finish(t, carry):
        d = pl.ds(pl.multiple_of(t * 64, 64), 64)
        total = accs[0][d, :]
        for acc in accs[1:]:
            total = total + acc[d, :]
        out_ref[d, :] = total
        return carry

    lax.fori_loop(0, voxels // 64, finish, 0)


def scatter(rows, index, voxels):
    q_count = rows.shape[0]
    return pl.pallas_call(
        functools.partial(scatter_kernel, q_count),
        out_shape=jax.ShapeDtypeStruct((voxels, 128), jnp.float32),
        in_specs=[
            pl.BlockSpec(memory_space=pltpu.VMEM),
            pl.BlockSpec(memory_space=pl.ANY),
        ],
        out_specs=pl.BlockSpec(memory_space=pltpu.VMEM),
        scratch_shapes=[pltpu.SMEM(index.shape, jnp.int32), pltpu.SemaphoreType.DMA]
        + [pltpu.VMEM((voxels, 128), jnp.float32)] * ACCS,
        compiler_params=pltpu.CompilerParams(vmem_limit_bytes=48 * 2**20),
    )(rows, index)


def local(counts, pixel_gain, slices, voxel_index, interp):
    voxels = VB_DEV * lax.axis_size("orient") * lax.axis_size("frame")
    rows, voxel_weight = iterate(counts, pixel_gain, interp, voxel_index, slices)
    voxel_sum = scatter(rows, voxel_index, voxels)
    return reduce_blocks(
        voxel_sum.reshape(SIDE, SIDE, SIDE, 2, VB_DEV, 128), voxel_weight.reshape(2, SIDE, SIDE * SIDE, 128)
    )


def solution(mesh):
    placed = (
        P(("orient", "frame"), None),
        P(),
        P("orient", None),
        P("orient", None),
        P("orient", None),
    )
    return jax.shard_map(
        local, mesh=mesh, in_specs=placed, out_specs=P(("orient", "frame"), None), check_vma=False
    )
```
